512 devices in a mesh: dp: 2 (over y_lo), ctx: 16 (over z), head: 16 (over y_hi, x, core).
Axes of the slice: x: 4, y: 4 (y_hi: 2, y_lo: 2; y = y_hi * 2 + y_lo), z: 16, core: 2. Of those that a mesh axis runs over, the one named last changes fastest.
Arguments:
- latent: bfloat16 [2, 2048, 576], P('dp', 'ctx'), may hold values from -8 to 8
- q_nope: bfloat16 [2, 2048, 8192], P('dp', 'ctx', 'head'), may hold values from -6 to 6
- q_rope: bfloat16 [2, 2048, 4096], P('dp', 'ctx', 'head'), may hold values from -8 to 8
- grad_out: bfloat16 [2, 2048, 8192], P('dp', 'ctx', 'head'), may hold values from -6 to 6
- w_uk: bfloat16 [512, 8192], P(None, 'head'), may hold values from -0.25 to 0.25
- w_uv: bfloat16 [512, 8192], P(None, 'head'), may hold values from -0.25 to 0.25
- stretch_order: int32 [32], replicated, may hold values from 0 to 31, as said below
Outputs:
- d_latent: float32 [2, 2048, 576], P('dp', ('ctx', 'head'))
- d_q_nope: bfloat16 [2, 2048, 8192], P('dp', 'ctx', 'head')
- d_q_rope: bfloat16 [2, 2048, 4096], P('dp', 'ctx', 'head')
- d_w_uk: float32 [512, 8192], P(None, 'head')
- d_w_uv: float32 [512, 8192], P(None, 'head')
The draws below stay inside these ranges and needn't reach their ends.
Inputs may be any that keep to these rules, and one draw needn't show every extreme that they name: `stretch_order`: entries 2d and 2d+1 name the causal blocks of the two row blocks of the d-th block of 128 rows; all entries together are a permutation, and each such pair sums to 31.
All inputs are finite; a program needn't handle non-finite values.
Results may differ from the reference program's by a relative error of at most 0.02.
Values may be sent and summed in bfloat16 or wider, within the bound.
No kernel may reach another device: no remote copies, remote signals or barrier semaphores. Data moves between devices by JAX's collectives and lax.ppermute only.
A program may use at most 64 MiB of HBM per device.

```python
import math
import jax
import jax.numpy as jnp
from jax import lax

D_LAT = 512
D_ROPE = 64
D_NOPE = 128
D_V = 128
HEADS_DEV = 4
TOK_DEV = 128
HEADS = 64
STRETCH = 64
SEQ = 2048
N_DP = 2
N_CTX = 16
N_HEAD = 16


def draw_latent(key, part):
    key = jax.random.fold_in(key, 1)
    width = D_LAT + D_ROPE
    base = jnp.clip(jax.random.normal(key, (N_DP, SEQ, width)), -8.0, 8.0)
    return base.astype(jnp.bfloat16)


def draw_q_rope(key, part):
    key = jax.random.fold_in(key, 2)
    width = HEADS * D_ROPE
    base = jnp.clip(jax.random.normal(key, (N_DP, SEQ, width)), -8.0, 8.0)
    return base.astype(jnp.bfloat16)


def draw_stretch_order(key, part):
    key = jax.random.fold_in(key, 3)
    low_stretches = jax.random.permutation(key, N_CTX).astype(jnp.int32)
    paired = jnp.stack([low_stretches, 2 * N_CTX - 1 - low_stretches], axis=1)
    return paired.reshape(2 * N_CTX).astype(jnp.int32)


def levels(stream_key, extent, split, low, high):
    loudness = 1.0
    for position, blocks in split:
        steps = jax.random.uniform(jax.random.fold_in(jax.random.fold_in(stream_key, 6), position), (blocks,), jnp.float32, low / len(split), high / len(split))
        loudness = loudness * jnp.repeat(jnp.exp(steps), extent[position] // blocks).reshape((-1,) + (1,) * (len(extent) - 1 - position))
    return loudness


def scatter_about(own_key, shape, deviation, bound, shards=(), kind=jnp.bfloat16):
    loudness = levels(own_key, shape, shards, -0.22, 0.18) if shards else 1.0
    drawn = jax.random.normal(own_key, shape, jnp.float32) * deviation * loudness
    return jnp.minimum(jnp.maximum(drawn, -bound), bound).astype(kind)


def setup_inputs(seed: int = 0) -> dict:
    streams_of = jax.random.split(jax.random.key(seed), 8)
    return {
        "latent": draw_latent(jax.random.fold_in(streams_of[7], 71), 0),
        "q_nope": scatter_about(streams_of[1], (N_DP, SEQ, HEADS * D_NOPE), 1.0, 6.0, ((0, 2), (1, 16), (2, 16))),
        "q_rope": draw_q_rope(jax.random.fold_in(streams_of[7], 71), 0),
        "grad_out": scatter_about(streams_of[3], (N_DP, SEQ, HEADS * D_V), 1.0, 6.0, ((0, 2), (1, 16), (2, 16))),
        "w_uk": scatter_about(streams_of[4], (D_LAT, HEADS * D_NOPE), D_LAT ** -0.5, 0.25, ((1, 16),)),
        "w_uv": scatter_about(streams_of[5], (D_LAT, HEADS * D_V), D_LAT ** -0.5, 0.25, ((1, 16),)),
        "stretch_order": draw_stretch_order(jax.random.fold_in(streams_of[7], 71), 0),
    }


def position_table(stretch_order):
    row_index = jnp.arange(SEQ, dtype=jnp.int32)
    slot_index = 2 * (row_index // TOK_DEV) + row_index % TOK_DEV // STRETCH
    return stretch_order[slot_index] * STRETCH + row_index % STRETCH

def head_terms(key_rows, query_nope, query_rope, grad_head, key_weight, value_weight, allowed):
    score_scale = 1.0 / math.sqrt(D_NOPE + D_ROPE)
    query_latent = jnp.dot(query_nope, key_weight.T, preferred_element_type=jnp.float32).astype(jnp.bfloat16)
    query_cat = jnp.concatenate([query_latent, query_rope], axis=1)
    grad_latent = jnp.dot(grad_head, value_weight.T, preferred_element_type=jnp.float32).astype(jnp.bfloat16)
    latent_part = key_rows[:, :D_LAT]
    raw_score = jnp.dot(query_cat, key_rows.T, preferred_element_type=jnp.float32) * score_scale
    raw_score = jnp.where(allowed, raw_score, -jnp.inf)
    probability = jax.nn.softmax(raw_score, axis=1)
    prob_grad = jnp.dot(grad_latent, latent_part.T, preferred_element_type=jnp.float32)
    row_delta = lax.optimization_barrier(jnp.sum(probability * prob_grad, axis=1, keepdims=True))
    prob_low = probability.astype(jnp.bfloat16)
    score_grad = (score_scale * probability * (prob_grad - row_delta)).astype(jnp.bfloat16)
    output_latent = jnp.dot(prob_low, latent_part, preferred_element_type=jnp.float32).astype(jnp.bfloat16)
    query_grad = jnp.dot(score_grad, key_rows, preferred_element_type=jnp.float32)
    latent_query = query_grad[:, :D_LAT].astype(jnp.bfloat16)
    rope_grad = query_grad[:, D_LAT:].astype(jnp.bfloat16)
    nope_grad = jnp.dot(latent_query, key_weight, preferred_element_type=jnp.float32).astype(jnp.bfloat16)
    key_update = jnp.dot(latent_query.T, query_nope, preferred_element_type=jnp.float32)
    value_update = jnp.dot(output_latent.T, grad_head, preferred_element_type=jnp.float32)
    block_score = score_grad.astype(jnp.float32).reshape(N_CTX, TOK_DEV, SEQ)
    block_query = query_cat.astype(jnp.float32).reshape(N_CTX, TOK_DEV, D_LAT + D_ROPE)
    key_side = jnp.einsum('dtk,dtf->dkf', block_score, block_query)
    block_prob = prob_low.astype(jnp.float32).reshape(N_CTX, TOK_DEV, SEQ)
    block_grad = grad_latent.astype(jnp.float32).reshape(N_CTX, TOK_DEV, D_LAT)
    value_side = jnp.einsum('dtk,dtf->dkf', block_prob, block_grad)
    key_side = key_side.at[:, :, :D_LAT].add(value_side)
    return (key_side, nope_grad, rope_grad, key_update, value_update)

def reference(latent, q_nope, q_rope, grad_out, w_uk, w_uv, stretch_order):
    positions = position_table(stretch_order)
    allowed = positions[None, :] <= positions[:, None]
    latent_list, nope_list, rope_list = ([], [], [])
    key_total = jnp.zeros((D_LAT, HEADS * D_NOPE), jnp.float32)
    value_total = jnp.zeros((D_LAT, HEADS * D_V), jnp.float32)
    for replica in range(N_DP):
        key_rows = latent[replica]

        def group_step(latent_sum, group_index, key_rows=key_rows, replica=replica):
            nope_cols = lax.dynamic_slice_in_dim(q_nope[replica], group_index * (HEADS_DEV * D_NOPE), HEADS_DEV * D_NOPE, 1)
            rope_cols = lax.dynamic_slice_in_dim(q_rope[replica], group_index * (HEADS_DEV * D_ROPE), HEADS_DEV * D_ROPE, 1)
            grad_cols = lax.dynamic_slice_in_dim(grad_out[replica], group_index * (HEADS_DEV * D_V), HEADS_DEV * D_V, 1)
            key_cols = lax.dynamic_slice_in_dim(w_uk, group_index * (HEADS_DEV * D_NOPE), HEADS_DEV * D_NOPE, 1)
            value_cols = lax.dynamic_slice_in_dim(w_uv, group_index * (HEADS_DEV * D_V), HEADS_DEV * D_V, 1)
            group_side = jnp.zeros((N_CTX, SEQ, D_LAT + D_ROPE), jnp.float32)
            nope_parts, rope_parts, key_parts, value_parts = ([], [], [], [])
            for member in range(HEADS_DEV):
                results = head_terms(key_rows, nope_cols[:, member * D_NOPE:(member + 1) * D_NOPE], rope_cols[:, member * D_ROPE:(member + 1) * D_ROPE], grad_cols[:, member * D_V:(member + 1) * D_V], key_cols[:, member * D_NOPE:(member + 1) * D_NOPE], value_cols[:, member * D_V:(member + 1) * D_V], allowed)
                group_side = group_side + results[0]
                nope_parts.append(results[1])
                rope_parts.append(results[2])
                key_parts.append(results[3])
                value_parts.append(results[4])
            rounded = lax.optimization_barrier(group_side.astype(jnp.bfloat16)).astype(jnp.float32)
            latent_sum = latent_sum + lax.optimization_barrier(jnp.sum(rounded, axis=0))
            stacked = (jnp.concatenate(nope_parts, axis=1), jnp.concatenate(rope_parts, axis=1), jnp.concatenate(key_parts, axis=1), jnp.concatenate(value_parts, axis=1))
            return (latent_sum, stacked)
        latent_sum, stacked = lax.scan(group_step, jnp.zeros((SEQ, D_LAT + D_ROPE), jnp.float32), jnp.arange(N_HEAD, dtype=jnp.int32))
        latent_list.append(latent_sum)
        nope_list.append(stacked[0].transpose(1, 0, 2).reshape(SEQ, HEADS * D_NOPE))
        rope_list.append(stacked[1].transpose(1, 0, 2).reshape(SEQ, HEADS * D_ROPE))
        key_total = key_total + stacked[2].transpose(1, 0, 2).reshape(D_LAT, HEADS * D_NOPE)
        value_total = value_total + stacked[3].transpose(1, 0, 2).reshape(D_LAT, HEADS * D_V)
    return (jnp.stack(latent_list), jnp.stack(nope_list), jnp.stack(rope_list), key_total, value_total)
```

```python
import math

import jax
import jax.numpy as jnp
from jax import lax
from jax.experimental import pallas as pl
from jax.experimental.pallas import tpu as pltpu
from jax.sharding import Mesh
from jax.sharding import PartitionSpec as P

D_LAT = 512
D_ROPE = 64
D_NOPE = 128
D_V = 128
KEY_WIDTH = D_LAT + D_ROPE
HEADS_DEV = 4
TOK_DEV = 128
STRETCH = 64
N_SLOT = 32
N_CTX = 16
ROWS = HEADS_DEV * STRETCH
CHUNK = 256
PER_CHUNK = CHUNK // STRETCH
STEPS = N_SLOT // PER_CHUNK + 1
SLICE = 8
NEG = -1e30
SCALE = 1.0 / math.sqrt(D_NOPE + D_ROPE)
LOG2E = 1.0 / math.log(2.0)
F32 = jnp.float32
BF16 = jnp.bfloat16
Z_AXES = ("zh", "z0")
PLANE = ("yh", "x")


def dot_nt(a, b):
    return lax.dot_general(a, b, (((1,), (1,)), ((), ())), preferred_element_type=F32)


def dot_tn(a, b):
    return lax.dot_general(a, b, (((0,), (0,)), ((), ())), preferred_element_type=F32)


def dot_nn(a, b):
    return lax.dot_general(a, b, (((1,), (0,)), ((), ())), preferred_element_type=F32)


def attention_kernel(
    order_ref,
    place_ref,
    own_ref,
    other_ref,
    qn_ref,
    qr_ref,
    go_ref,
    wk_ref,
    wv_ref,
    g_own_ref,
    g_other_ref,
    nope_ref,
    rope_ref,
    dw_ref,
    keys,
    query,
    grad,
    score,
    prob_grad,
    side,
    out_sum,
    query_sum,
    gap,
):
    ctx = place_ref[0]
    core = place_ref[1]
    first = order_ref[2 * ctx]
    second = order_ref[2 * ctx + 1]

    for slot in range(N_SLOT):
        block, upper = slot // 2, slot % 2
        rows = jnp.concatenate(
            [own_ref[upper, :, block].astype(F32), other_ref[upper, :, block].astype(F32)], axis=0
        )
        keys[order_ref[slot]] = rows.reshape(STRETCH, KEY_WIDTH).astype(BF16)

    for head in range(HEADS_DEV):
        cols = slice(head * D_NOPE, (head + 1) * D_NOPE)
        q_lat = dot_nt(qn_ref[:, cols], wk_ref[:, cols]).astype(BF16)
        g_lat = dot_nt(go_ref[:, cols], wv_ref[:, cols]).astype(BF16)
        for half in range(2):
            toks = slice(half * STRETCH, (half + 1) * STRETCH)
            into = slice(head * STRETCH, (head + 1) * STRETCH)
            query[half, into, :D_LAT] = q_lat[toks]
            query[half, into, D_LAT:] = qr_ref[toks, head * D_ROPE : (head + 1) * D_ROPE]
            grad[half, into, :] = g_lat[toks]

    col = lax.broadcasted_iota(jnp.int32, (ROWS, CHUNK), 1)
    row = lax.broadcasted_iota(jnp.int32, (ROWS, CHUNK), 0)
    within = col % STRETCH
    side_of = (within // 32 + core) % 2
    key_pos = (col // STRETCH) * STRETCH + ((within % 32) // SLICE) * 16 + side_of * SLICE + within % SLICE
    gap[...] = key_pos - row % STRETCH

    count = first // PER_CHUNK + 1
    zero_col = jnp.zeros((ROWS, 1), F32)

    def place_of(step):
        half = jnp.where(step >= count, 1, 0)
        return half, step - half * count

    def chunk_of(ref, chunk):
        return ref[pl.ds(chunk * PER_CHUNK, PER_CHUNK)].reshape(CHUNK, KEY_WIDTH)

    tops = []
    for step in range(STEPS):
        half, chunk = place_of(step)
        key_rows = chunk_of(keys, chunk)
        limit = jnp.where(half == 1, second, first) * STRETCH - chunk * CHUNK
        raw = dot_nt(query[half], key_rows) * (SCALE * LOG2E)
        raw = jnp.where(gap[...] <= limit, raw, NEG)
        score[step] = raw
        prob_grad[step] = dot_nt(grad[half], key_rows[:, :D_LAT])
        tops.append(jnp.max(raw, axis=1, keepdims=True))

    def by_half(values, join, start):
        sums = [start, start]
        for step, value in enumerate(values):
            in_first = step < count
            sums[0] = join(sums[0], jnp.where(in_first, value, start))
            sums[1] = join(sums[1], jnp.where(in_first, start, value))
        return sums

    top = by_half(tops, jnp.maximum, zero_col + NEG)
    totals, weights = [], []
    for step in range(STEPS):
        expo = jnp.exp2(score[step] - jnp.where(step < count, top[0], top[1]))
        score[step] = expo
        totals.append(jnp.sum(expo, axis=1, keepdims=True))
        weights.append(jnp.sum(expo * prob_grad[step], axis=1, keepdims=True))
    total = by_half(totals, jnp.add, zero_col)
    weight = by_half(weights, jnp.add, zero_col)
    inverse = [1.0 / total[0], 1.0 / total[1]]
    delta = [weight[0] * inverse[0], weight[1] * inverse[1]]

    side[...] = jnp.zeros_like(side)
    out_sum[...] = jnp.zeros_like(out_sum)
    query_sum[...] = jnp.zeros_like(query_sum)
    for step in range(STEPS):
        half, chunk = place_of(step)
        in_first = step < count
        key_rows = chunk_of(keys, chunk)
        probability = score[step] * jnp.where(in_first, inverse[0], inverse[1])
        prob_low = probability.astype(BF16)
        drift = prob_grad[step] - jnp.where(in_first, delta[0], delta[1])
        score_grad = (SCALE * probability * drift).astype(BF16)
        out_sum[half] += dot_nn(prob_low, key_rows[:, :D_LAT])
        query_sum[half] += dot_nn(score_grad, key_rows)
        where = pl.ds(chunk * PER_CHUNK, PER_CHUNK)
        key_side = dot_tn(score_grad, query[half]).reshape(PER_CHUNK, STRETCH, KEY_WIDTH)
        value_side = dot_tn(prob_low, grad[half]).reshape(PER_CHUNK, STRETCH, D_LAT)
        side[where] += key_side
        side[where, :, :D_LAT] += value_side

    for head in range(HEADS_DEV):
        cols = slice(head * D_NOPE, (head + 1) * D_NOPE)
        into = slice(head * STRETCH, (head + 1) * STRETCH)
        query_low = jnp.concatenate([query_sum[0, into, :], query_sum[1, into, :]], axis=0).astype(BF16)
        out_low = jnp.concatenate([out_sum[0, into, :], out_sum[1, into, :]], axis=0).astype(BF16)
        lat_low = query_low[:, :D_LAT]
        rope_ref[:, head * D_ROPE : (head + 1) * D_ROPE] = query_low[:, D_LAT:]
        nope_ref[:, cols] = dot_nn(lat_low, wk_ref[:, cols]).astype(BF16)
        dw_ref[:D_LAT, cols] = dot_tn(lat_low, qn_ref[:, cols]).astype(BF16)
        dw_ref[D_LAT:, cols] = dot_tn(out_low, go_ref[:, cols]).astype(BF16)

    for slot in range(N_SLOT):
        block, upper = slot // 2, slot % 2
        rows = side[order_ref[slot]].reshape(2, 4, SLICE, KEY_WIDTH).astype(BF16)
        g_own_ref[upper, :, block] = rows[0]
        g_other_ref[upper, :, block] = rows[1]


def attention(order, place, own, other, qn, qr, go, wk, wv):
    vmem = pl.BlockSpec(memory_space=pltpu.VMEM)
    smem = pl.BlockSpec(memory_space=pltpu.SMEM)
    part = jax.ShapeDtypeStruct(own.shape, BF16)
    return pl.pallas_call(
        attention_kernel,
        out_shape=(
            part,
            part,
            jax.ShapeDtypeStruct((TOK_DEV, HEADS_DEV * D_NOPE), BF16),
            jax.ShapeDtypeStruct((TOK_DEV, HEADS_DEV * D_ROPE), BF16),
            jax.ShapeDtypeStruct((2 * D_LAT, HEADS_DEV * D_NOPE), BF16),
        ),
        in_specs=[smem, smem] + [vmem] * 7,
        out_specs=(vmem,) * 5,
        scratch_shapes=[
            pltpu.VMEM((N_SLOT, STRETCH, KEY_WIDTH), BF16),
            pltpu.VMEM((2, ROWS, KEY_WIDTH), BF16),
            pltpu.VMEM((2, ROWS, D_LAT), BF16),
            pltpu.VMEM((STEPS, ROWS, CHUNK), F32),
            pltpu.VMEM((STEPS, ROWS, CHUNK), F32),
            pltpu.VMEM((N_SLOT, STRETCH, KEY_WIDTH), F32),
            pltpu.VMEM((2, ROWS, D_LAT), F32),
            pltpu.VMEM((2, ROWS, KEY_WIDTH), F32),
            pltpu.VMEM((ROWS, CHUNK), jnp.int32),
        ],
        compiler_params=pltpu.CompilerParams(vmem_limit_bytes=48 * 1024 * 1024),
        name="latent_attention",
    )(order, place, own, other, qn, qr, go, wk, wv)


def swap(values, axes):
    return lax.all_to_all(values, axes, 0, 0, tiled=True)


def local(latent, q_nope, q_rope, grad_out, w_uk, w_uv, stretch_order):
    ctx = lax.axis_index(Z_AXES)
    core = lax.axis_index("c")
    head = lax.axis_index(PLANE + ("c",))
    other_core = [(0, 1), (1, 0)]
    place = jnp.stack([ctx, core]).astype(jnp.int32)

    mine = lax.dynamic_slice_in_dim(latent[0], head * SLICE, SLICE, 0)
    column = swap(jnp.broadcast_to(mine, (N_CTX, SLICE, KEY_WIDTH)), Z_AXES)
    own = swap(jnp.broadcast_to(column, (8, N_CTX, SLICE, KEY_WIDTH)), PLANE)
    own = own.reshape(2, 4, N_CTX, SLICE, KEY_WIDTH)
    other = lax.ppermute(own, "c", other_core)

    g_own, g_other, nope_grad, rope_grad, dw = attention(
        stretch_order, place, own, other, q_nope[0], q_rope[0], grad_out[0], w_uk, w_uv
    )

    came = lax.ppermute(g_other, "c", other_core)
    pair = (g_own.astype(F32) + came.astype(F32)).astype(BF16)
    planes = swap(pair.reshape(8, N_CTX, SLICE, KEY_WIDTH), PLANE)
    plane_sum = jnp.sum(planes.astype(F32), axis=0).astype(BF16)

    corners = swap(dw.reshape(4, 256, 512), ("dp", "z0"))
    quarter = jnp.sum(corners.astype(F32), axis=0).astype(BF16).reshape(N_CTX, 16, 512)

    packed = jnp.concatenate(
        [
            quarter,
            plane_sum[:, :, :D_LAT],
            plane_sum[:, :, D_LAT:].reshape(N_CTX, 1, SLICE * D_ROPE),
        ],
        axis=1,
    )
    columns = swap(packed, Z_AXES).astype(F32)
    owned = jnp.sum(columns[:, 16:], axis=0)
    d_latent = jnp.concatenate([owned[:8], owned[8].reshape(SLICE, D_ROPE)], axis=1)
    pieces = jnp.sum(columns[:, :16].reshape(8, 2, 16, 512), axis=0).astype(BF16)

    whole = swap(jnp.broadcast_to(pieces, (8, 2, 16, 512)).reshape(N_CTX, 16, 512), Z_AXES)
    whole = swap(jnp.broadcast_to(whole.reshape(256, 512), (4, 256, 512)), ("dp", "z0"))
    whole = whole.reshape(1024, 512).astype(F32)
    return (
        d_latent[None],
        nope_grad[None],
        rope_grad[None],
        whole[:D_LAT],
        whole[D_LAT:],
    )


def solution(mesh):
    fine = Mesh(mesh.devices.reshape(2, 8, 2, 2, 4, 2), ("dp", "zh", "z0", "yh", "x", "c"))
    heads = ("yh", "x", "c")
    placed = (
        P("dp", Z_AXES, None),
        P("dp", Z_AXES, heads),
        P("dp", Z_AXES, heads),
        P("dp", Z_AXES, heads),
        P(None, heads),
        P(None, heads),
        P(),
    )
    return jax.shard_map(
        local,
        mesh=fine,
        in_specs=placed,
        out_specs=(
            P("dp", Z_AXES + heads, None),
            P("dp", Z_AXES, heads),
            P("dp", Z_AXES, heads),
            P(None, heads),
            P(None, heads),
        ),
        check_vma=False,
    )
```

```python
import math

import jax
import jax.numpy as jnp
from jax import lax
from jax.experimental import pallas as pl
from jax.experimental.pallas import tpu as pltpu
from jax.sharding import Mesh
from jax.sharding import PartitionSpec as P

D_LAT = 512
D_ROPE = 64
D_NOPE = 128
D_V = 128
KEY_WIDTH = D_LAT + D_ROPE
HEADS_DEV = 4
TOK_DEV = 128
STRETCH = 64
N_SLOT = 32
N_CTX = 16
TEAM = 4
ROWS = TEAM * STRETCH
CHUNK = 256
PER_CHUNK = CHUNK // STRETCH
CHUNKS = N_SLOT // PER_CHUNK
LOW_CHUNKS = CHUNKS // 2
STEPS = CHUNKS + LOW_CHUNKS
SENT = D_NOPE + D_V + 128
SLICE = 8
NEG = -1e30
SCALE = 1.0 / math.sqrt(D_NOPE + D_ROPE)
LOG2E = 1.0 / math.log(2.0)
F32 = jnp.float32
BF16 = jnp.bfloat16
Z_AXES = ("zq", "z1", "z0")
PLANE = ("yh", "x")


def dot_nt(a, b):
    return lax.dot_general(a, b, (((1,), (1,)), ((), ())), preferred_element_type=F32)


def dot_tn(a, b):
    return lax.dot_general(a, b, (((0,), (0,)), ((), ())), preferred_element_type=F32)


def dot_nn(a, b):
    return lax.dot_general(a, b, (((1,), (0,)), ((), ())), preferred_element_type=F32)


def scaled(index, unit):
    return pl.ds(pl.multiple_of(index * unit, unit), unit)


def member(place_ref, ahead):
    return (place_ref[0] % TEAM) ^ ahead


def low_half(order_ref, place_ref, ahead):
    block = place_ref[0] ^ ahead
    return jnp.where(order_ref[2 * block] > order_ref[2 * block + 1], 1, 0)


def split_kernel(place_ref, qn_ref, qr_ref, go_ref, *out_refs):
    for ahead, out_ref in enumerate(out_refs):
        head = member(place_ref, ahead)
        out_ref[:, :D_NOPE] = qn_ref[:, scaled(head, D_NOPE)]
        out_ref[:, D_NOPE : D_NOPE + D_V] = go_ref[:, scaled(head, D_V)]
        two = qr_ref[:, scaled(head // 2, 2 * D_ROPE)]
        one = jnp.where(head % 2 == 1, two[:, D_ROPE:].astype(F32), two[:, :D_ROPE].astype(F32))
        out_ref[:, D_NOPE + D_V : D_NOPE + D_V + D_ROPE] = one.astype(BF16)
        out_ref[:, D_NOPE + D_V + D_ROPE :] = jnp.zeros((TOK_DEV, D_ROPE), BF16)


def prepare_kernel(order_ref, place_ref, *refs):
    rows_refs, (wk_ref, wv_ref, query, grad, qn, go) = refs[:TEAM], refs[TEAM:]
    head = scaled(member(place_ref, 0), D_NOPE)
    wk, wv = wk_ref[:, head], wv_ref[:, head]
    for ahead, rows_ref in enumerate(rows_refs):
        nope, out = rows_ref[:, :D_NOPE], rows_ref[:, D_NOPE : D_NOPE + D_V]
        rope = rows_ref[:, D_NOPE + D_V : D_NOPE + D_V + D_ROPE]
        q_lat = dot_nt(nope, wk).astype(BF16)
        g_lat = dot_nt(out, wv).astype(BF16)
        late = low_half(order_ref, place_ref, ahead)
        into = slice(ahead * STRETCH, (ahead + 1) * STRETCH)
        for half in range(2):
            toks = slice(half * STRETCH, (half + 1) * STRETCH)
            group = half ^ late
            query[group, into, :D_LAT] = q_lat[toks]
            query[group, into, D_LAT:] = rope[toks]
            grad[group, into, :] = g_lat[toks]
            qn[group, into, :] = nope[toks]
            go[group, into, :] = out[toks]


def score_kernel(
    order_ref,
    place_ref,
    own_ref,
    other_ref,
    query,
    grad,
    prob_ref,
    score_grad_ref,
    keys,
    score,
    prob_grad,
):
    @pl.loop(0, N_CTX, unroll=4)
    def _(block):
        for upper in range(2):
            rows = jnp.concatenate(
                [own_ref[upper, :, block].astype(F32), other_ref[upper, :, block].astype(F32)], axis=0
            )
            keys[order_ref[2 * block + upper]] = rows.reshape(STRETCH, KEY_WIDTH).astype(BF16)

    col = lax.broadcasted_iota(jnp.int32, (1, CHUNK), 1)
    within = col % STRETCH
    side_of = (within // 32 + place_ref[1]) % 2
    key_pos = (col // STRETCH) * STRETCH + ((within % 32) // SLICE) * 16 + side_of * SLICE + within % SLICE

    row = lax.broadcasted_iota(jnp.int32, (ROWS, 1), 0)
    row_pos = [row % STRETCH, row % STRETCH]
    for ahead in range(TEAM):
        block = place_ref[0] ^ ahead
        first, second = order_ref[2 * block], order_ref[2 * block + 1]
        mine = row // STRETCH == ahead
        row_pos[0] += jnp.where(mine, jnp.minimum(first, second) * STRETCH, 0)
        row_pos[1] += jnp.where(mine, jnp.maximum(first, second) * STRETCH, 0)

    for group in range(2):
        first_step, chunks = (0, LOW_CHUNKS) if group == 0 else (LOW_CHUNKS, CHUNKS)
        top = jnp.full((ROWS, 1), NEG, F32)
        for chunk in range(chunks):
            cols = slice((first_step + chunk) * CHUNK, (first_step + chunk + 1) * CHUNK)
            key_rows = keys[chunk * PER_CHUNK : (chunk + 1) * PER_CHUNK].reshape(CHUNK, KEY_WIDTH)
            raw = dot_nt(query[group], key_rows) * (SCALE * LOG2E)
            if group == 0 or chunk >= LOW_CHUNKS:
                raw = jnp.where(key_pos + chunk * CHUNK <= row_pos[group], raw, NEG)
            score[:, cols] = raw
            prob_grad[:, cols] = dot_nt(grad[group], key_rows[:, :D_LAT])
            top = jnp.maximum(top, jnp.max(raw, axis=1, keepdims=True))
        total = jnp.zeros((ROWS, 1), F32)
        weight = jnp.zeros((ROWS, 1), F32)
        for chunk in range(chunks):
            cols = slice((first_step + chunk) * CHUNK, (first_step + chunk + 1) * CHUNK)
            expo = jnp.exp2(score[:, cols] - top)
            score[:, cols] = expo
            total += jnp.sum(expo, axis=1, keepdims=True)
            weight += jnp.sum(expo * prob_grad[:, cols], axis=1, keepdims=True)
        inverse = 1.0 / total
        delta = weight * inverse
        for chunk in range(chunks):
            cols = slice((first_step + chunk) * CHUNK, (first_step + chunk + 1) * CHUNK)
            probability = score[:, cols] * inverse
            prob_ref[:, cols] = probability.astype(BF16)
            score_grad_ref[:, cols] = (SCALE * probability * (prob_grad[:, cols] - delta)).astype(BF16)


def query_kernel(
    order_ref,
    place_ref,
    keys,
    prob_ref,
    score_grad_ref,
    qn_ref,
    go_ref,
    wk_ref,
    dw_ref,
    *refs,
):
    rows_refs, (query_low, out_low, nope) = refs[:TEAM], refs[TEAM:]
    for group in range(2):
        cols = slice(0, LOW_CHUNKS * CHUNK) if group == 0 else slice(LOW_CHUNKS * CHUNK, STEPS * CHUNK)
        count = N_SLOT // 2 if group == 0 else N_SLOT
        key_rows = keys[:count].reshape(count * STRETCH, KEY_WIDTH)
        out_low[group] = dot_nn(prob_ref[:, cols], key_rows[:, :D_LAT]).astype(BF16)
        query_low[group] = dot_nn(score_grad_ref[:, cols], key_rows).astype(BF16)

    wk = wk_ref[:, scaled(member(place_ref, 0), D_NOPE)]
    lat_low = query_low[:, :, :D_LAT].reshape(2 * ROWS, D_LAT)
    dw_ref[0] = dot_tn(lat_low, qn_ref[...].reshape(2 * ROWS, D_NOPE)).astype(BF16)
    dw_ref[1] = dot_tn(out_low[...].reshape(2 * ROWS, D_LAT), go_ref[...].reshape(2 * ROWS, D_V)).astype(BF16)
    nope[...] = dot_nn(lat_low, wk).astype(BF16).reshape(2, ROWS, D_NOPE)
    for ahead, rows_ref in enumerate(rows_refs):
        late = low_half(order_ref, place_ref, ahead)
        rows = slice(ahead * STRETCH, (ahead + 1) * STRETCH)
        for half in range(2):
            toks = slice(half * STRETCH, (half + 1) * STRETCH)
            group = half ^ late
            rows_ref[toks, :D_NOPE] = nope[group, rows]
            rows_ref[toks, D_NOPE:] = query_low[group, rows, D_LAT:]


def heads_kernel(place_ref, *refs):
    rows_refs, (nope_ref, rope_ref, store) = refs[:TEAM], refs[TEAM:]
    for ahead, rows_ref in enumerate(rows_refs):
        store[member(place_ref, ahead)] = rows_ref[...]
    for head in range(TEAM):
        nope_ref[:, head * D_NOPE : (head + 1) * D_NOPE] = store[head, :, :D_NOPE]
        rope_ref[:, head * D_ROPE : (head + 1) * D_ROPE] = store[head, :, D_NOPE:]


def side_kernel(
    order_ref, place_ref, query, grad, prob_ref, score_grad_ref, g_own_ref, g_other_ref, side
):
    both_query = query[...].reshape(2 * ROWS, KEY_WIDTH)
    both_grad = grad[...].reshape(2 * ROWS, D_LAT)
    for chunk in range(CHUNKS):
        late = slice((LOW_CHUNKS + chunk) * CHUNK, (LOW_CHUNKS + chunk + 1) * CHUNK)
        early = slice(chunk * CHUNK, (chunk + 1) * CHUNK)
        where = slice(chunk * PER_CHUNK, (chunk + 1) * PER_CHUNK)
        if chunk < LOW_CHUNKS:
            score_grad = jnp.concatenate([score_grad_ref[:, early], score_grad_ref[:, late]], axis=0)
            prob = jnp.concatenate([prob_ref[:, early], prob_ref[:, late]], axis=0)
            key_side, value_side = dot_tn(score_grad, both_query), dot_tn(prob, both_grad)
        else:
            key_side = dot_tn(score_grad_ref[:, late], query[1])
            value_side = dot_tn(prob_ref[:, late], grad[1])
        lat = key_side[:, :D_LAT] + value_side
        side[where, :, :D_LAT] = lat.reshape(PER_CHUNK, STRETCH, D_LAT)
        side[where, :, D_LAT:] = key_side[:, D_LAT:].reshape(PER_CHUNK, STRETCH, D_ROPE)

    @pl.loop(0, N_CTX, unroll=4)
    def _(block):
        for upper in range(2):
            rows = side[order_ref[2 * block + upper]].reshape(2, 4, SLICE, KEY_WIDTH).astype(BF16)
            apart = (upper + place_ref[2]) % 2
            for line in range(4):
                ahead = (line + 4 - place_ref[3]) % 4
                g_own_ref[ahead, apart, block] = rows[0, line]
                g_other_ref[ahead, apart, block] = rows[1, line]


def pair_kernel(own_ref, came_ref, *out_refs):
    for ahead, out_ref in enumerate(out_refs):
        out_ref[...] = (own_ref[ahead].astype(F32) + came_ref[ahead].astype(F32)).astype(BF16)


def line_kernel(a_ref, b_ref, c_ref, d_ref, keep_ref, give_ref):
    for apart, out_ref in enumerate((keep_ref, give_ref)):
        total = a_ref[apart].astype(F32) + b_ref[apart].astype(F32)
        total += c_ref[apart].astype(F32) + d_ref[apart].astype(F32)
        out_ref[...] = total.astype(BF16)


def pack_kernel(columns_ref, keep_ref, came_ref, out_ref):
    pieces = []
    for head in range(TEAM):
        total = columns_ref[head].astype(F32)
        for source in range(head + TEAM, 2 * N_CTX, TEAM):
            total += columns_ref[source].astype(F32)
        pieces.append(total)
    for target in range(N_CTX):
        for pick in range(2):
            piece = pieces[2 * pick + target % 2]
            for octet in range(4):
                lanes = slice((4 * pick + octet) * 128, (4 * pick + octet + 1) * 128)
                out_ref[target, :, lanes] = piece[octet * SLICE : (octet + 1) * SLICE].astype(BF16)
    side = keep_ref[...].astype(F32) + came_ref[...].astype(F32)
    out_ref[:, :, 1024:] = side.astype(BF16)


def spread_kernel(whole_ref, key_ref, value_ref):
    for corner in range(4):
        out_ref, parity = (key_ref, value_ref)[corner // 2], corner % 2
        for source in range(N_CTX):
            for pick in range(2):
                head = 2 * pick + parity
                for octet in range(4):
                    lanes = slice((4 * pick + octet) * 128, (4 * pick + octet + 1) * 128)
                    rows = slice(source * 32 + octet * SLICE, source * 32 + (octet + 1) * SLICE)
                    out_ref[rows, head * 128 : (head + 1) * 128] = whole_ref[corner, source, :, lanes].astype(F32)


VMEM = pl.BlockSpec(memory_space=pltpu.VMEM)
SMEM = pl.BlockSpec(memory_space=pltpu.SMEM)


def call(kernel, name, n_smem, args, outs, scratch=(), flops=2**20, moved=2**20, dtype=BF16):
    shapes = tuple(jax.ShapeDtypeStruct(shape, dtype) for shape in outs)
    return pl.pallas_call(
        kernel,
        out_shape=shapes,
        in_specs=[SMEM] * n_smem + [VMEM] * (len(args) - n_smem),
        out_specs=(VMEM,) * len(outs),
        scratch_shapes=list(scratch),
        compiler_params=pltpu.CompilerParams(vmem_limit_bytes=24 * 1024 * 1024),
        cost_estimate=pl.CostEstimate(flops=flops, bytes_accessed=moved, transcendentals=0),
        name=name,
    )(*args)


QUERY_SHAPE = (2, ROWS, KEY_WIDTH)
GRAD_SHAPE = (2, ROWS, D_LAT)
HEAD_SHAPE = (2, ROWS, D_NOPE)
STEP_SHAPE = (ROWS, STEPS * CHUNK)


def split(place, qn, qr, go):
    return call(split_kernel, "split_heads", 1, (place, qn, qr, go), ((TOK_DEV, SENT),) * TEAM)


def prepare(order, place, rows, wk, wv):
    outs = (QUERY_SHAPE, GRAD_SHAPE, HEAD_SHAPE, HEAD_SHAPE)
    return call(prepare_kernel, "query_latents", 2, (order, place, *rows, wk, wv), outs, (), 2**28, 2**21)


def scores(order, place, own, other, query, grad):
    return call(
        score_kernel,
        "scores",
        2,
        (order, place, own, other, query, grad),
        (STEP_SHAPE, STEP_SHAPE, (N_SLOT, STRETCH, KEY_WIDTH)),
        [pltpu.VMEM(STEP_SHAPE, F32), pltpu.VMEM(STEP_SHAPE, F32)],
        2**31,
        2**23,
    )


def query_side(order, place, keys, prob, score_grad, qn, go, wk):
    rows = (TOK_DEV, D_NOPE + D_ROPE)
    return call(
        query_kernel,
        "query_side",
        2,
        (order, place, keys, prob, score_grad, qn, go, wk),
        ((2, D_LAT, D_NOPE),) + (rows,) * TEAM,
        [pltpu.VMEM(QUERY_SHAPE, BF16), pltpu.VMEM(GRAD_SHAPE, BF16), pltpu.VMEM(HEAD_SHAPE, BF16)],
        2**31,
        2**23,
    )


def put_heads(place, rows):
    return call(
        heads_kernel,
        "put_heads",
        1,
        (place, *rows),
        ((TOK_DEV, TEAM * D_NOPE), (TOK_DEV, TEAM * D_ROPE)),
        [pltpu.VMEM((TEAM, TOK_DEV, D_NOPE + D_ROPE), BF16)],
    )


def side_sums(order, place, query, grad, prob, score_grad):
    part = (4, 2, N_CTX, SLICE, KEY_WIDTH)
    return call(
        side_kernel,
        "key_side",
        2,
        (order, place, query, grad, prob, score_grad),
        (part, part),
        [pltpu.VMEM((N_SLOT, STRETCH, KEY_WIDTH), F32)],
        2**31,
        2**23,
    )


def swap(values, axes):
    return lax.all_to_all(values, axes, 0, 0, tiled=True)


def flip(values, axis):
    return lax.ppermute(values, axis, [(0, 1), (1, 0)])


def team_swap(parts):
    moved = [parts[0]]
    for ahead in range(1, TEAM):
        moved.append(lax.ppermute(parts[ahead], ("z1", "z0"), [(i, i ^ ahead) for i in range(TEAM)]))
    return moved


def local(latent, q_nope, q_rope, grad_out, w_uk, w_uv, stretch_order):
    head = lax.axis_index(PLANE + ("c",))
    places = (Z_AXES, "c", "yh", "x")
    place = jnp.stack([lax.axis_index(axis) for axis in places]).astype(jnp.int32)

    mine = lax.dynamic_slice_in_dim(latent[0], head * SLICE, SLICE, 0)
    column = swap(jnp.broadcast_to(mine, (N_CTX, SLICE, KEY_WIDTH)), Z_AXES)
    own = swap(jnp.broadcast_to(column, (8, N_CTX, SLICE, KEY_WIDTH)), PLANE)
    rows = team_swap(split(place, q_nope[0], q_rope[0], grad_out[0]))
    own, *rows = lax.optimization_barrier((own, *rows))
    query, grad, qn, go = prepare(stretch_order, place, rows, w_uk, w_uv)
    own = own.reshape(2, 4, N_CTX, SLICE, KEY_WIDTH)
    other = flip(own, "c")

    prob, score_grad, keys = scores(stretch_order, place, own, other, query, grad)
    g_own, g_other = side_sums(stretch_order, place, query, grad, prob, score_grad)
    came = flip(g_other, "c")
    prob, g_own = lax.optimization_barrier((prob, g_own))
    dw, *rows = query_side(stretch_order, place, keys, prob, score_grad, qn, go, w_uk)

    half = (2, N_CTX, SLICE, KEY_WIDTH)
    parts = call(pair_kernel, "pair_sum", 0, (g_own, came), (half,) * 4)
    dw, *parts = lax.optimization_barrier((dw, *parts))
    lines = [parts[0]]
    for ahead in (1, 3, 2):
        lines.append(lax.ppermute(parts[ahead], "x", [(i, (i + ahead) % 4) for i in range(4)]))

    columns = swap(dw.reshape(2 * N_CTX, 32, D_NOPE), ("dp", *Z_AXES))

    keep, give = call(line_kernel, "line_sum", 0, lines, (half[1:],) * 2)
    came = flip(give, "yh")
    (packed,) = call(pack_kernel, "pack", 0, (columns, keep, came), ((N_CTX, SLICE, 1024 + KEY_WIDTH),))
    packed = swap(packed, Z_AXES)
    nope_grad, rope_grad = put_heads(place, team_swap(rows))
    d_latent = jnp.sum(packed[:, :, 1024:].astype(F32), axis=0)
    whole = swap(jnp.broadcast_to(packed[:, :, :1024], (4, N_CTX, SLICE, 1024)), ("dp", "z0"))
    wide = (D_LAT, HEADS_DEV * D_NOPE)
    key_weight, value_weight = call(spread_kernel, "spread", 0, (whole,), (wide, wide), dtype=F32)
    return (d_latent[None], nope_grad[None], rope_grad[None], key_weight, value_weight)


def solution(mesh):
    fine = Mesh(mesh.devices.reshape(2, 4, 2, 2, 2, 4, 2), ("dp", *Z_AXES, "yh", "x", "c"))
    heads = ("yh", "x", "c")
    placed = (
        P("dp", Z_AXES, None),
        P("dp", Z_AXES, heads),
        P("dp", Z_AXES, heads),
        P("dp", Z_AXES, heads),
        P(None, heads),
        P(None, heads),
        P(),
    )
    return jax.shard_map(
        local,
        mesh=fine,
        in_specs=placed,
        out_specs=(
            P("dp", Z_AXES + heads, None),
            P("dp", Z_AXES, heads),
            P("dp", Z_AXES, heads),
            P(None, heads),
            P(None, heads),
        ),
        check_vma=False,
    )
```

```python
import math

import jax
import jax.numpy as jnp
from jax import lax
from jax.experimental import pallas as pl
from jax.experimental.pallas import tpu as pltpu
from jax.sharding import Mesh
from jax.sharding import PartitionSpec as P

D_LAT = 512
D_ROPE = 64
D_NOPE = 128
D_V = 128
KEY_WIDTH = D_LAT + D_ROPE
HEADS_DEV = 4
TOK_DEV = 128
STRETCH = 64
N_SLOT = 32
N_CTX = 16
TEAM = 4
ROWS = TEAM * STRETCH
CHUNK = 256
PER_CHUNK = CHUNK // STRETCH
CHUNKS = N_SLOT // PER_CHUNK
LOW_CHUNKS = CHUNKS // 2
STEPS = CHUNKS + LOW_CHUNKS
SENT = D_NOPE + D_V + 128
SLICE = 8
NEG = -1e30
SCALE = 1.0 / math.sqrt(D_NOPE + D_ROPE)
LOG2E = 1.0 / math.log(2.0)
F32 = jnp.float32
BF16 = jnp.bfloat16
Z_AXES = ("zq", "z1", "z0")
PLANE = ("yh", "x")


def dot_nt(a, b):
    return lax.dot_general(a, b, (((1,), (1,)), ((), ())), preferred_element_type=F32)


def dot_tn(a, b):
    return lax.dot_general(a, b, (((0,), (0,)), ((), ())), preferred_element_type=F32)


def dot_nn(a, b):
    return lax.dot_general(a, b, (((1,), (0,)), ((), ())), preferred_element_type=F32)


def scaled(index, unit):
    return pl.ds(pl.multiple_of(index * unit, unit), unit)


def member(place_ref, ahead):
    return (place_ref[0] % TEAM) ^ ahead


def low_half(order_ref, place_ref, ahead):
    block = place_ref[0] ^ ahead
    return jnp.where(order_ref[2 * block] > order_ref[2 * block + 1], 1, 0)


def split_kernel(place_ref, qn_ref, qr_ref, go_ref, *out_refs):
    for ahead, out_ref in enumerate(out_refs):
        head = member(place_ref, ahead)
        out_ref[:, :D_NOPE] = qn_ref[:, scaled(head, D_NOPE)]
        out_ref[:, D_NOPE : D_NOPE + D_V] = go_ref[:, scaled(head, D_V)]
        two = qr_ref[:, scaled(head // 2, 2 * D_ROPE)]
        one = jnp.where(head % 2 == 1, two[:, D_ROPE:].astype(F32), two[:, :D_ROPE].astype(F32))
        out_ref[:, D_NOPE + D_V : D_NOPE + D_V + D_ROPE] = one.astype(BF16)
        out_ref[:, D_NOPE + D_V + D_ROPE :] = jnp.zeros((TOK_DEV, D_ROPE), BF16)


def prepare_kernel(order_ref, place_ref, *refs):
    rows_refs, (wk_ref, wv_ref, query, grad, qn, go) = refs[:TEAM], refs[TEAM:]
    head = scaled(member(place_ref, 0), D_NOPE)
    wk, wv = wk_ref[:, head], wv_ref[:, head]
    for ahead, rows_ref in enumerate(rows_refs):
        nope, out = rows_ref[:, :D_NOPE], rows_ref[:, D_NOPE : D_NOPE + D_V]
        rope = rows_ref[:, D_NOPE + D_V : D_NOPE + D_V + D_ROPE]
        q_lat = dot_nt(nope, wk).astype(BF16)
        g_lat = dot_nt(out, wv).astype(BF16)
        late = low_half(order_ref, place_ref, ahead)
        into = slice(ahead * STRETCH, (ahead + 1) * STRETCH)
        for half in range(2):
            toks = slice(half * STRETCH, (half + 1) * STRETCH)
            group = half ^ late
            query[group, into, :D_LAT] = q_lat[toks]
            query[group, into, D_LAT:] = rope[toks]
            grad[group, into, :] = g_lat[toks]
            qn[group, into, :] = nope[toks]
            go[group, into, :] = out[toks]


def score_kernel(
    order_ref,
    place_ref,
    own_ref,
    other_ref,
    query,
    grad,
    prob_ref,
    score_grad_ref,
    keys,
    score,
    prob_grad,
):
    @pl.loop(0, N_CTX, unroll=4)
    def _(block):
        for upper in range(2):
            rows = jnp.concatenate(
                [own_ref[upper, :, block].astype(F32), other_ref[upper, :, block].astype(F32)], axis=0
            )
            keys[order_ref[2 * block + upper]] = rows.reshape(STRETCH, KEY_WIDTH).astype(BF16)

    col = lax.broadcasted_iota(jnp.int32, (1, CHUNK), 1)
    within = col % STRETCH
    side_of = (within // 32 + place_ref[1]) % 2
    key_pos = (col // STRETCH) * STRETCH + ((within % 32) // SLICE) * 16 + side_of * SLICE + within % SLICE

    row = lax.broadcasted_iota(jnp.int32, (ROWS, 1), 0)
    row_pos = [row % STRETCH, row % STRETCH]
    for ahead in range(TEAM):
        block = place_ref[0] ^ ahead
        first, second = order_ref[2 * block], order_ref[2 * block + 1]
        mine = row // STRETCH == ahead
        row_pos[0] += jnp.where(mine, jnp.minimum(first, second) * STRETCH, 0)
        row_pos[1] += jnp.where(mine, jnp.maximum(first, second) * STRETCH, 0)

    for group in range(2):
        first_step, chunks = (0, LOW_CHUNKS) if group == 0 else (LOW_CHUNKS, CHUNKS)
        top = jnp.full((ROWS, 1), NEG, F32)
        for chunk in range(chunks):
            cols = slice((first_step + chunk) * CHUNK, (first_step + chunk + 1) * CHUNK)
            key_rows = keys[chunk * PER_CHUNK : (chunk + 1) * PER_CHUNK].reshape(CHUNK, KEY_WIDTH)
            raw = dot_nt(query[group], key_rows) * (SCALE * LOG2E)
            if group == 0 or chunk >= LOW_CHUNKS:
                raw = jnp.where(key_pos + chunk * CHUNK <= row_pos[group], raw, NEG)
            score[:, cols] = raw
            prob_grad[:, cols] = dot_nt(grad[group], key_rows[:, :D_LAT])
            top = jnp.maximum(top, jnp.max(raw, axis=1, keepdims=True))
        total = jnp.zeros((ROWS, 1), F32)
        weight = jnp.zeros((ROWS, 1), F32)
        for chunk in range(chunks):
            cols = slice((first_step + chunk) * CHUNK, (first_step + chunk + 1) * CHUNK)
            expo = jnp.exp2(score[:, cols] - top)
            score[:, cols] = expo
            total += jnp.sum(expo, axis=1, keepdims=True)
            weight += jnp.sum(expo * prob_grad[:, cols], axis=1, keepdims=True)
        inverse = 1.0 / total
        delta = weight * inverse
        for chunk in range(chunks):
            cols = slice((first_step + chunk) * CHUNK, (first_step + chunk + 1) * CHUNK)
            probability = score[:, cols] * inverse
            prob_ref[:, cols] = probability.astype(BF16)
            score_grad_ref[:, cols] = (SCALE * probability * (prob_grad[:, cols] - delta)).astype(BF16)


def query_kernel(
    order_ref,
    place_ref,
    keys,
    prob_ref,
    score_grad_ref,
    qn_ref,
    go_ref,
    wk_ref,
    keep_ref,
    give_ref,
    *refs,
):
    rows_refs, (query_low, out_low, nope) = refs[:TEAM], refs[TEAM:]
    for group in range(2):
        cols = slice(0, LOW_CHUNKS * CHUNK) if group == 0 else slice(LOW_CHUNKS * CHUNK, STEPS * CHUNK)
        count = N_SLOT // 2 if group == 0 else N_SLOT
        key_rows = keys[:count].reshape(count * STRETCH, KEY_WIDTH)
        out_low[group] = dot_nn(prob_ref[:, cols], key_rows[:, :D_LAT]).astype(BF16)
        query_low[group] = dot_nn(score_grad_ref[:, cols], key_rows).astype(BF16)

    wk = wk_ref[:, scaled(member(place_ref, 0), D_NOPE)]
    lat_low = query_low[:, :, :D_LAT].reshape(2 * ROWS, D_LAT)
    key_weight = dot_tn(lat_low, qn_ref[...].reshape(2 * ROWS, D_NOPE))
    value_weight = dot_tn(out_low[...].reshape(2 * ROWS, D_LAT), go_ref[...].reshape(2 * ROWS, D_V))
    even = place_ref[3] == 0
    keep_ref[...] = jnp.where(even, key_weight, value_weight).astype(BF16)
    give_ref[...] = jnp.where(even, value_weight, key_weight).astype(BF16)
    nope[...] = dot_nn(lat_low, wk).astype(BF16).reshape(2, ROWS, D_NOPE)
    for ahead, rows_ref in enumerate(rows_refs):
        late = low_half(order_ref, place_ref, ahead)
        rows = slice(ahead * STRETCH, (ahead + 1) * STRETCH)
        for half in range(2):
            toks = slice(half * STRETCH, (half + 1) * STRETCH)
            group = half ^ late
            rows_ref[toks, :D_NOPE] = nope[group, rows]
            rows_ref[toks, D_NOPE:] = query_low[group, rows, D_LAT:]


def heads_kernel(place_ref, *refs):
    rows_refs, (nope_ref, rope_ref, store) = refs[:TEAM], refs[TEAM:]
    for ahead, rows_ref in enumerate(rows_refs):
        store[member(place_ref, ahead)] = rows_ref[...]
    for head in range(TEAM):
        nope_ref[:, head * D_NOPE : (head + 1) * D_NOPE] = store[head, :, :D_NOPE]
        rope_ref[:, head * D_ROPE : (head + 1) * D_ROPE] = store[head, :, D_NOPE:]


def side_kernel(
    order_ref, place_ref, query, grad, prob_ref, score_grad_ref, g_own_ref, g_other_ref, side
):
    both_query = query[...].reshape(2 * ROWS, KEY_WIDTH)
    both_grad = grad[...].reshape(2 * ROWS, D_LAT)
    for chunk in range(CHUNKS):
        late = slice((LOW_CHUNKS + chunk) * CHUNK, (LOW_CHUNKS + chunk + 1) * CHUNK)
        early = slice(chunk * CHUNK, (chunk + 1) * CHUNK)
        where = slice(chunk * PER_CHUNK, (chunk + 1) * PER_CHUNK)
        if chunk < LOW_CHUNKS:
            score_grad = jnp.concatenate([score_grad_ref[:, early], score_grad_ref[:, late]], axis=0)
            prob = jnp.concatenate([prob_ref[:, early], prob_ref[:, late]], axis=0)
            key_side, value_side = dot_tn(score_grad, both_query), dot_tn(prob, both_grad)
        else:
            key_side = dot_tn(score_grad_ref[:, late], query[1])
            value_side = dot_tn(prob_ref[:, late], grad[1])
        lat = key_side[:, :D_LAT] + value_side
        side[where, :, :D_LAT] = lat.reshape(PER_CHUNK, STRETCH, D_LAT)
        side[where, :, D_LAT:] = key_side[:, D_LAT:].reshape(PER_CHUNK, STRETCH, D_ROPE)

    @pl.loop(0, N_CTX, unroll=4)
    def _(block):
        for upper in range(2):
            rows = side[order_ref[2 * block + upper]].reshape(2, 4, SLICE, KEY_WIDTH).astype(BF16)
            apart = (upper + place_ref[2]) % 2
            for line in range(4):
                g_own_ref[line, apart, block] = rows[0, line]
                g_other_ref[line, apart, block] = rows[1, line]


def pair_kernel(own_ref, came_ref, out_ref):
    total = own_ref[...].astype(F32) + came_ref[...].astype(F32)
    out_ref[...] = total.astype(BF16)


def line_kernel(lines_ref, keep_ref, give_ref):
    for apart, out_ref in enumerate((keep_ref, give_ref)):
        total = lines_ref[0, apart].astype(F32)
        for source in range(1, 4):
            total += lines_ref[source, apart].astype(F32)
        out_ref[...] = total.astype(BF16)


def weight_kernel(keep_ref, came_ref, out_ref):
    total = keep_ref[...].astype(F32) + came_ref[...].astype(F32)
    out_ref[...] = total.astype(BF16).reshape(out_ref.shape)


def pack_kernel(columns_ref, keep_ref, came_ref, out_ref):
    pieces = []
    for head in range(TEAM):
        total = columns_ref[head].astype(F32)
        for source in range(head + TEAM, N_CTX, TEAM):
            total += columns_ref[source].astype(F32)
        pieces.append(total)
    for target in range(N_CTX):
        for pick in range(2):
            piece = pieces[2 * pick + target % 2]
            for octet in range(4):
                lanes = slice((4 * pick + octet) * 128, (4 * pick + octet + 1) * 128)
                out_ref[target, :, lanes] = piece[octet * SLICE : (octet + 1) * SLICE].astype(BF16)
    side = keep_ref[...].astype(F32) + came_ref[...].astype(F32)
    out_ref[:, :, 1024:] = side.astype(BF16)


def spread_kernel(whole_ref, key_ref, value_ref):
    for corner in range(4):
        out_ref, parity = (key_ref, value_ref)[corner // 2], corner % 2
        for source in range(N_CTX):
            for pick in range(2):
                head = 2 * pick + parity
                for octet in range(4):
                    lanes = slice((4 * pick + octet) * 128, (4 * pick + octet + 1) * 128)
                    rows = slice(source * 32 + octet * SLICE, source * 32 + (octet + 1) * SLICE)
                    out_ref[rows, head * 128 : (head + 1) * 128] = whole_ref[corner, source, :, lanes].astype(F32)


VMEM = pl.BlockSpec(memory_space=pltpu.VMEM)
SMEM = pl.BlockSpec(memory_space=pltpu.SMEM)


def call(kernel, name, n_smem, args, outs, scratch=(), flops=2**20, moved=2**20, dtype=BF16):
    shapes = tuple(jax.ShapeDtypeStruct(shape, dtype) for shape in outs)
    return pl.pallas_call(
        kernel,
        out_shape=shapes,
        in_specs=[SMEM] * n_smem + [VMEM] * (len(args) - n_smem),
        out_specs=(VMEM,) * len(outs),
        scratch_shapes=list(scratch),
        compiler_params=pltpu.CompilerParams(vmem_limit_bytes=24 * 1024 * 1024),
        cost_estimate=pl.CostEstimate(flops=flops, bytes_accessed=moved, transcendentals=0),
        name=name,
    )(*args)


QUERY_SHAPE = (2, ROWS, KEY_WIDTH)
GRAD_SHAPE = (2, ROWS, D_LAT)
HEAD_SHAPE = (2, ROWS, D_NOPE)
STEP_SHAPE = (ROWS, STEPS * CHUNK)


def split(place, qn, qr, go):
    return call(split_kernel, "split_heads", 1, (place, qn, qr, go), ((TOK_DEV, SENT),) * TEAM)


def prepare(order, place, rows, wk, wv):
    outs = (QUERY_SHAPE, GRAD_SHAPE, HEAD_SHAPE, HEAD_SHAPE)
    return call(prepare_kernel, "query_latents", 2, (order, place, *rows, wk, wv), outs, (), 2**28, 2**21)


def scores(order, place, own, other, query, grad):
    return call(
        score_kernel,
        "scores",
        2,
        (order, place, own, other, query, grad),
        (STEP_SHAPE, STEP_SHAPE, (N_SLOT, STRETCH, KEY_WIDTH)),
        [pltpu.VMEM(STEP_SHAPE, F32), pltpu.VMEM(STEP_SHAPE, F32)],
        2**31,
        2**23,
    )


def query_side(order, place, keys, prob, score_grad, qn, go, wk):
    rows = (TOK_DEV, D_NOPE + D_ROPE)
    return call(
        query_kernel,
        "query_side",
        2,
        (order, place, keys, prob, score_grad, qn, go, wk),
        ((D_LAT, D_NOPE), (D_LAT, D_NOPE)) + (rows,) * TEAM,
        [pltpu.VMEM(QUERY_SHAPE, BF16), pltpu.VMEM(GRAD_SHAPE, BF16), pltpu.VMEM(HEAD_SHAPE, BF16)],
        2**31,
        2**23,
    )


def put_heads(place, rows):
    return call(
        heads_kernel,
        "put_heads",
        1,
        (place, *rows),
        ((TOK_DEV, TEAM * D_NOPE), (TOK_DEV, TEAM * D_ROPE)),
        [pltpu.VMEM((TEAM, TOK_DEV, D_NOPE + D_ROPE), BF16)],
    )


def side_sums(order, place, query, grad, prob, score_grad):
    part = (4, 2, N_CTX, SLICE, KEY_WIDTH)
    return call(
        side_kernel,
        "key_side",
        2,
        (order, place, query, grad, prob, score_grad),
        (part, part),
        [pltpu.VMEM((N_SLOT, STRETCH, KEY_WIDTH), F32)],
        2**31,
        2**23,
    )


def swap(values, axes):
    return lax.all_to_all(values, axes, 0, 0, tiled=True)


def flip(values, axis):
    return lax.ppermute(values, axis, [(0, 1), (1, 0)])


def team_swap(parts):
    moved = [parts[0]]
    for ahead in range(1, TEAM):
        moved.append(lax.ppermute(parts[ahead], ("z1", "z0"), [(i, i ^ ahead) for i in range(TEAM)]))
    return moved


def local(latent, q_nope, q_rope, grad_out, w_uk, w_uv, stretch_order):
    head = lax.axis_index(PLANE + ("c",))
    places = (Z_AXES, "c", "yh", "dp")
    place = jnp.stack([lax.axis_index(axis) for axis in places]).astype(jnp.int32)

    mine = lax.dynamic_slice_in_dim(latent[0], head * SLICE, SLICE, 0)
    column = swap(jnp.broadcast_to(mine, (N_CTX, SLICE, KEY_WIDTH)), Z_AXES)
    own = swap(jnp.broadcast_to(column, (8, N_CTX, SLICE, KEY_WIDTH)), PLANE)
    rows = team_swap(split(place, q_nope[0], q_rope[0], grad_out[0]))
    own, *rows = lax.optimization_barrier((own, *rows))
    query, grad, qn, go = prepare(stretch_order, place, rows, w_uk, w_uv)
    own = own.reshape(2, 4, N_CTX, SLICE, KEY_WIDTH)
    other = flip(own, "c")

    prob, score_grad, keys = scores(stretch_order, place, own, other, query, grad)
    g_own, g_other = side_sums(stretch_order, place, query, grad, prob, score_grad)
    came = flip(g_other, "c")
    prob, g_own = lax.optimization_barrier((prob, g_own))
    keep, give, *rows = query_side(stretch_order, place, keys, prob, score_grad, qn, go, w_uk)

    (pair,) = call(pair_kernel, "pair_sum", 0, (g_own, came), (g_own.shape,))
    give, pair = lax.optimization_barrier((give, pair))
    lines = swap(pair, "x")
    (weights,) = call(weight_kernel, "weight_sum", 0, (keep, flip(give, "dp")), ((N_CTX, 32, D_NOPE),))
    rows = team_swap(rows)
    lines, weights, rows = lax.optimization_barrier((lines, weights, rows))
    keep, give = call(line_kernel, "line_sum", 0, (lines,), (pair.shape[2:],) * 2)
    give, weights = lax.optimization_barrier((give, weights))
    columns = swap(weights, Z_AXES)
    came = flip(give, "yh")
    (packed,) = call(pack_kernel, "pack", 0, (columns, keep, came), ((N_CTX, SLICE, 1024 + KEY_WIDTH),))
    packed = swap(packed, Z_AXES)
    nope_grad, rope_grad = put_heads(place, rows)
    d_latent = jnp.sum(packed[:, :, 1024:].astype(F32), axis=0)
    whole = swap(jnp.broadcast_to(packed[:, :, :1024], (4, N_CTX, SLICE, 1024)), ("dp", "z0"))
    wide = (D_LAT, HEADS_DEV * D_NOPE)
    key_weight, value_weight = call(spread_kernel, "spread", 0, (whole,), (wide, wide), dtype=F32)
    return (d_latent[None], nope_grad[None], rope_grad[None], key_weight, value_weight)


def solution(mesh):
    fine = Mesh(mesh.devices.reshape(2, 4, 2, 2, 2, 4, 2), ("dp", *Z_AXES, "yh", "x", "c"))
    heads = ("yh", "x", "c")
    placed = (
        P("dp", Z_AXES, None),
        P("dp", Z_AXES, heads),
        P("dp", Z_AXES, heads),
        P("dp", Z_AXES, heads),
        P(None, heads),
        P(None, heads),
        P(),
    )
    return jax.shard_map(
        local,
        mesh=fine,
        in_specs=placed,
        out_specs=(
            P("dp", Z_AXES + heads, None),
            P("dp", Z_AXES, heads),
            P("dp", Z_AXES, heads),
            P(None, heads),
            P(None, heads),
        ),
        check_vma=False,
    )
```

```python
import math

import jax
import jax.numpy as jnp
from jax import lax
from jax.experimental import pallas as pl
from jax.experimental.pallas import tpu as pltpu
from jax.sharding import Mesh
from jax.sharding import PartitionSpec as P

D_LAT = 512
D_ROPE = 64
D_NOPE = 128
D_V = 128
KEY_WIDTH = D_LAT + D_ROPE
HEADS_DEV = 4
TOK_DEV = 128
STRETCH = 64
N_SLOT = 32
N_CTX = 16
TEAM = 4
ROWS = TEAM * STRETCH
CHUNK = 256
HALF = STRETCH // 2
PER_CHUNK = CHUNK // HALF
CHUNKS = N_SLOT // PER_CHUNK
LOW_CHUNKS = CHUNKS // 2
STEPS = CHUNKS + LOW_CHUNKS
PAIRS = N_CTX // 2
WIDE = 2 * KEY_WIDTH
SENT = D_NOPE + D_V + 128
SLICE = 8
NEG = -1e30
SCALE = 1.0 / math.sqrt(D_NOPE + D_ROPE)
LOG2E = 1.0 / math.log(2.0)
F32 = jnp.float32
BF16 = jnp.bfloat16
Z_AXES = ("zq", "z1", "z0")
PLANE = ("yh", "x")


def dot_nt(a, b):
    return lax.dot_general(a, b, (((1,), (1,)), ((), ())), preferred_element_type=F32)


def dot_tn(a, b):
    return lax.dot_general(a, b, (((0,), (0,)), ((), ())), preferred_element_type=F32)


def dot_nn(a, b):
    return lax.dot_general(a, b, (((1,), (0,)), ((), ())), preferred_element_type=F32)


def scaled(index, unit):
    return pl.ds(pl.multiple_of(index * unit, unit), unit)


def member(place_ref, ahead):
    return (place_ref[0] % TEAM) ^ ahead


def low_half(order_ref, place_ref, ahead):
    block = place_ref[0] ^ ahead
    return jnp.where(order_ref[2 * block] > order_ref[2 * block + 1], 1, 0)


def lat_lanes(parity):
    return slice(parity * D_LAT, (parity + 1) * D_LAT)


def rope_lanes(parity):
    return slice(2 * D_LAT + parity * D_ROPE, 2 * D_LAT + (parity + 1) * D_ROPE)


def split_kernel(place_ref, qn_ref, qr_ref, go_ref, *out_refs):
    for ahead, out_ref in enumerate(out_refs):
        head = member(place_ref, ahead)
        out_ref[:, :D_NOPE] = qn_ref[:, scaled(head, D_NOPE)]
        out_ref[:, D_NOPE : D_NOPE + D_V] = go_ref[:, scaled(head, D_V)]
        two = qr_ref[:, scaled(head // 2, 2 * D_ROPE)]
        one = jnp.where(head % 2 == 1, two[:, D_ROPE:].astype(F32), two[:, :D_ROPE].astype(F32))
        out_ref[:, D_NOPE + D_V : D_NOPE + D_V + D_ROPE] = one.astype(BF16)
        out_ref[:, D_NOPE + D_V + D_ROPE :] = jnp.zeros((TOK_DEV, D_ROPE), BF16)


def prepare_kernel(order_ref, place_ref, *refs):
    rows_refs, (wk_ref, wv_ref, query, grad, qn, go) = refs[:TEAM], refs[TEAM:]
    head = scaled(member(place_ref, 0), D_NOPE)
    wk, wv = wk_ref[:, head], wv_ref[:, head]
    for ahead, rows_ref in enumerate(rows_refs):
        nope, out = rows_ref[:, :D_NOPE], rows_ref[:, D_NOPE : D_NOPE + D_V]
        rope = rows_ref[:, D_NOPE + D_V : D_NOPE + D_V + D_ROPE]
        q_lat = dot_nt(nope, wk).astype(BF16)
        g_lat = dot_nt(out, wv).astype(BF16)
        late = low_half(order_ref, place_ref, ahead)
        into = slice(ahead * STRETCH, (ahead + 1) * STRETCH)
        for half in range(2):
            toks = slice(half * STRETCH, (half + 1) * STRETCH)
            group = half ^ late
            query[group, into, :D_LAT] = q_lat[toks]
            query[group, into, D_LAT:] = rope[toks]
            grad[group, into, :] = g_lat[toks]
            qn[group, into, :] = nope[toks]
            go[group, into, :] = out[toks]


def step_lanes(group, chunk):
    step = chunk if group == 0 else LOW_CHUNKS + chunk
    return slice(step * CHUNK, (step + 1) * CHUNK)


def group_chunks(group):
    return LOW_CHUNKS if group == 0 else CHUNKS


def half_scores(order_ref, place_ref, half, rows_ref, query, grad, keys, score, prob_grad):
    @pl.loop(0, PAIRS, unroll=4)
    def _(pair):
        for upper in range(2):
            rows = rows_ref[upper, :, pair].astype(F32).reshape(HALF, WIDE).astype(BF16)
            for parity in range(2):
                place = order_ref[4 * pair + 2 * parity + upper]
                keys[place, :, :D_LAT] = rows[:, lat_lanes(parity)]
                keys[place, :, D_LAT:] = rows[:, rope_lanes(parity)]

    col = lax.broadcasted_iota(jnp.int32, (1, CHUNK), 1)
    within = col % HALF
    core = (place_ref[1] + half) % 2
    key_pos = (col // HALF) * STRETCH + (within // SLICE) * 16 + core * SLICE + within % SLICE

    row = lax.broadcasted_iota(jnp.int32, (ROWS, 1), 0)
    row_pos = [row % STRETCH, row % STRETCH]
    for ahead in range(TEAM):
        block = place_ref[0] ^ ahead
        first, second = order_ref[2 * block], order_ref[2 * block + 1]
        mine = row // STRETCH == ahead
        row_pos[0] += jnp.where(mine, jnp.minimum(first, second) * STRETCH, 0)
        row_pos[1] += jnp.where(mine, jnp.maximum(first, second) * STRETCH, 0)

    tops = []
    for group in range(2):
        top = jnp.full((ROWS, 1), NEG, F32)
        for chunk in range(group_chunks(group)):
            lanes = step_lanes(group, chunk)
            key_rows = keys[chunk * PER_CHUNK : (chunk + 1) * PER_CHUNK].reshape(CHUNK, KEY_WIDTH)
            raw = dot_nt(query[group], key_rows) * (SCALE * LOG2E)
            if group == 0 or chunk >= LOW_CHUNKS:
                raw = jnp.where(key_pos + chunk * PER_CHUNK * STRETCH <= row_pos[group], raw, NEG)
            score[:, lanes] = raw
            prob_grad[:, lanes] = dot_nt(grad[group], key_rows[:, :D_LAT])
            top = jnp.maximum(top, jnp.max(raw, axis=1, keepdims=True))
        tops.append(top)
    return tops


def own_kernel(order_ref, place_ref, own_ref, query, grad, keys, score, prob_grad, top_ref):
    tops = half_scores(order_ref, place_ref, 0, own_ref, query, grad, keys, score, prob_grad)
    for group in range(2):
        top_ref[group] = jnp.broadcast_to(tops[group], (ROWS, 128))


def score_kernel(
    order_ref,
    place_ref,
    other_ref,
    query,
    grad,
    own_score,
    own_prob_grad,
    top_ref,
    keys,
    prob_ref,
    score_grad_ref,
    score,
    prob_grad,
    expo_ref,
):
    tops = half_scores(order_ref, place_ref, 1, other_ref, query, grad, keys, score, prob_grad)
    halves = ((own_score, own_prob_grad), (score, prob_grad))
    for group in range(2):
        top = jnp.maximum(tops[group], top_ref[group, :, :1])
        total = jnp.zeros((ROWS, 1), F32)
        weight = jnp.zeros((ROWS, 1), F32)
        for half, (raw_ref, grad_ref) in enumerate(halves):
            for chunk in range(group_chunks(group)):
                lanes = step_lanes(group, chunk)
                expo = jnp.exp2(raw_ref[:, lanes] - top)
                expo_ref[half, :, lanes] = expo
                total += jnp.sum(expo, axis=1, keepdims=True)
                weight += jnp.sum(expo * grad_ref[:, lanes], axis=1, keepdims=True)
        inverse = 1.0 / total
        delta = weight * inverse
        for half, (raw_ref, grad_ref) in enumerate(halves):
            for chunk in range(group_chunks(group)):
                lanes = step_lanes(group, chunk)
                probability = expo_ref[half, :, lanes] * inverse
                prob_ref[half, :, lanes] = probability.astype(BF16)
                drift = grad_ref[:, lanes] - delta
                score_grad_ref[half, :, lanes] = (SCALE * probability * drift).astype(BF16)


def query_kernel(
    order_ref,
    place_ref,
    own_keys,
    other_keys,
    prob_ref,
    score_grad_ref,
    qn_ref,
    go_ref,
    wk_ref,
    keep_ref,
    give_ref,
    *refs,
):
    rows_refs, (query_low, out_low, nope) = refs[:TEAM], refs[TEAM:]
    for group in range(2):
        lanes = slice(0, LOW_CHUNKS * CHUNK) if group == 0 else slice(LOW_CHUNKS * CHUNK, STEPS * CHUNK)
        count = group_chunks(group) * PER_CHUNK
        out, query_grad = [], []
        for half, keys in enumerate((own_keys, other_keys)):
            key_rows = keys[:count].reshape(count * HALF, KEY_WIDTH)
            out.append(dot_nn(prob_ref[half, :, lanes], key_rows[:, :D_LAT]))
            query_grad.append(dot_nn(score_grad_ref[half, :, lanes], key_rows))
        out_low[group] = (out[0] + out[1]).astype(BF16)
        query_low[group] = (query_grad[0] + query_grad[1]).astype(BF16)

    wk = wk_ref[:, scaled(member(place_ref, 0), D_NOPE)]
    lat_low = query_low[:, :, :D_LAT].reshape(2 * ROWS, D_LAT)
    key_weight = dot_tn(lat_low, qn_ref[...].reshape(2 * ROWS, D_NOPE))
    value_weight = dot_tn(out_low[...].reshape(2 * ROWS, D_LAT), go_ref[...].reshape(2 * ROWS, D_V))
    even = place_ref[3] == 0
    keep_ref[...] = jnp.where(even, key_weight, value_weight).astype(BF16)
    give_ref[...] = jnp.where(even, value_weight, key_weight).astype(BF16)
    nope[...] = dot_nn(lat_low, wk).astype(BF16).reshape(2, ROWS, D_NOPE)
    for ahead, rows_ref in enumerate(rows_refs):
        late = low_half(order_ref, place_ref, ahead)
        rows = slice(ahead * STRETCH, (ahead + 1) * STRETCH)
        for half in range(2):
            toks = slice(half * STRETCH, (half + 1) * STRETCH)
            group = half ^ late
            rows_ref[toks, :D_NOPE] = nope[group, rows]
            rows_ref[toks, D_NOPE:] = query_low[group, rows, D_LAT:]


def heads_kernel(place_ref, *refs):
    rows_refs, (nope_ref, rope_ref, store) = refs[:TEAM], refs[TEAM:]
    for ahead, rows_ref in enumerate(rows_refs):
        store[member(place_ref, ahead)] = rows_ref[...]
    for head in range(TEAM):
        nope_ref[:, head * D_NOPE : (head + 1) * D_NOPE] = store[head, :, :D_NOPE]
        rope_ref[:, head * D_ROPE : (head + 1) * D_ROPE] = store[head, :, D_NOPE:]


def side_kernel(
    order_ref, place_ref, query, grad, prob_ref, score_grad_ref, g_own_ref, g_other_ref, side
):
    both_query = query[...].reshape(2 * ROWS, KEY_WIDTH)
    both_grad = grad[...].reshape(2 * ROWS, D_LAT)
    for half in range(2):
        for chunk in range(CHUNKS):
            late, where = step_lanes(1, chunk), slice(chunk * PER_CHUNK, (chunk + 1) * PER_CHUNK)
            if chunk < LOW_CHUNKS:
                early = step_lanes(0, chunk)
                score_grad, prob = [
                    jnp.concatenate([ref[half, :, early], ref[half, :, late]], axis=0)
                    for ref in (score_grad_ref, prob_ref)
                ]
                key_side, value_side = dot_tn(score_grad, both_query), dot_tn(prob, both_grad)
            else:
                key_side = dot_tn(score_grad_ref[half, :, late], query[1])
                value_side = dot_tn(prob_ref[half, :, late], grad[1])
            lat = key_side[:, :D_LAT] + value_side
            side[half, where, :, :D_LAT] = lat.reshape(PER_CHUNK, HALF, D_LAT)
            side[half, where, :, D_LAT:] = key_side[:, D_LAT:].reshape(PER_CHUNK, HALF, D_ROPE)

    @pl.loop(0, PAIRS, unroll=4)
    def _(pair):
        for upper in range(2):
            apart = (upper + place_ref[2]) % 2
            for half, out_ref in enumerate((g_own_ref, g_other_ref)):
                both = [side[half, order_ref[4 * pair + 2 * parity + upper]] for parity in range(2)]
                rows = jnp.concatenate(
                    [both[0][:, :D_LAT], both[1][:, :D_LAT], both[0][:, D_LAT:], both[1][:, D_LAT:]], axis=1
                )
                out_ref[:, apart, pair] = rows.reshape(4, SLICE, WIDE).astype(BF16)


def pair_kernel(own_ref, came_ref, out_ref):
    total = own_ref[...].astype(F32) + came_ref[...].astype(F32)
    out_ref[...] = total.astype(BF16)


def line_kernel(lines_ref, keep_ref, give_ref):
    for apart, out_ref in enumerate((keep_ref, give_ref)):
        total = lines_ref[0, apart].astype(F32)
        for source in range(1, 4):
            total += lines_ref[source, apart].astype(F32)
        out_ref[...] = total.astype(BF16)


def weight_kernel(keep_ref, came_ref, out_ref):
    total = keep_ref[...].astype(F32) + came_ref[...].astype(F32)
    out_ref[...] = total.astype(BF16).reshape(out_ref.shape)


def pack_kernel(columns_ref, keep_ref, came_ref, out_ref):
    pieces = []
    for head in range(TEAM):
        total = columns_ref[head].astype(F32)
        for source in range(head + TEAM, N_CTX, TEAM):
            total += columns_ref[source].astype(F32)
        pieces.append(total)
    for target in range(N_CTX):
        for pick in range(2):
            piece = pieces[2 * pick + target % 2]
            for octet in range(4):
                lanes = slice((4 * pick + octet) * 128, (4 * pick + octet + 1) * 128)
                out_ref[target, :, lanes] = piece[octet * SLICE : (octet + 1) * SLICE].astype(BF16)
    side = (keep_ref[...].astype(F32) + came_ref[...].astype(F32)).astype(BF16)
    for pair in range(PAIRS):
        for parity in range(2):
            out_ref[2 * pair + parity, :, 1024 : 1024 + D_LAT] = side[pair, :, lat_lanes(parity)]
            out_ref[2 * pair + parity, :, 1024 + D_LAT :] = side[pair, :, rope_lanes(parity)]


def spread_kernel(whole_ref, key_ref, value_ref):
    for corner in range(4):
        out_ref, parity = (key_ref, value_ref)[corner // 2], corner % 2
        for source in range(N_CTX):
            for pick in range(2):
                head = 2 * pick + parity
                for octet in range(4):
                    lanes = slice((4 * pick + octet) * 128, (4 * pick + octet + 1) * 128)
                    rows = slice(source * 32 + octet * SLICE, source * 32 + (octet + 1) * SLICE)
                    out_ref[rows, head * 128 : (head + 1) * 128] = whole_ref[corner, source, :, lanes].astype(F32)


VMEM = pl.BlockSpec(memory_space=pltpu.VMEM)
SMEM = pl.BlockSpec(memory_space=pltpu.SMEM)


def call(kernel, name, n_smem, args, outs, scratch=(), flops=2**20, moved=2**20, dtype=BF16):
    types = dtype if isinstance(dtype, tuple) else (dtype,) * len(outs)
    shapes = tuple(jax.ShapeDtypeStruct(shape, kind) for shape, kind in zip(outs, types))
    return pl.pallas_call(
        kernel,
        out_shape=shapes,
        in_specs=[SMEM] * n_smem + [VMEM] * (len(args) - n_smem),
        out_specs=(VMEM,) * len(outs),
        scratch_shapes=list(scratch),
        compiler_params=pltpu.CompilerParams(vmem_limit_bytes=24 * 1024 * 1024),
        cost_estimate=pl.CostEstimate(flops=flops, bytes_accessed=moved, transcendentals=0),
        name=name,
    )(*args)


QUERY_SHAPE = (2, ROWS, KEY_WIDTH)
GRAD_SHAPE = (2, ROWS, D_LAT)
HEAD_SHAPE = (2, ROWS, D_NOPE)
STEP_SHAPE = (ROWS, STEPS * CHUNK)
KEY_SHAPE = (N_SLOT, HALF, KEY_WIDTH)


def split(place, qn, qr, go):
    return call(split_kernel, "split_heads", 1, (place, qn, qr, go), ((TOK_DEV, SENT),) * TEAM)


def prepare(order, place, rows, wk, wv):
    outs = (QUERY_SHAPE, GRAD_SHAPE, HEAD_SHAPE, HEAD_SHAPE)
    return call(prepare_kernel, "query_latents", 2, (order, place, *rows, wk, wv), outs, (), 2**28, 2**21)


def own_scores(order, place, own, query, grad):
    args = (order, place, own, query, grad)
    outs = (KEY_SHAPE, STEP_SHAPE, STEP_SHAPE, (2, ROWS, 128))
    return call(own_kernel, "own_scores", 2, args, outs, (), 2**30, 2**22, (BF16, F32, F32, F32))


def scores(order, place, other, query, grad, own):
    args = (order, place, other, query, grad, *own)
    outs = (KEY_SHAPE, (2, *STEP_SHAPE), (2, *STEP_SHAPE))
    scratch = [pltpu.VMEM(STEP_SHAPE, F32), pltpu.VMEM(STEP_SHAPE, F32), pltpu.VMEM((2, *STEP_SHAPE), F32)]
    return call(score_kernel, "scores", 2, args, outs, scratch, 2**31, 2**23)


def query_side(order, place, own_keys, keys, prob, score_grad, qn, go, wk):
    rows = (TOK_DEV, D_NOPE + D_ROPE)
    return call(
        query_kernel,
        "query_side",
        2,
        (order, place, own_keys, keys, prob, score_grad, qn, go, wk),
        ((D_LAT, D_NOPE), (D_LAT, D_NOPE)) + (rows,) * TEAM,
        [pltpu.VMEM(QUERY_SHAPE, BF16), pltpu.VMEM(GRAD_SHAPE, BF16), pltpu.VMEM(HEAD_SHAPE, BF16)],
        2**31,
        2**23,
    )


def put_heads(place, rows):
    return call(
        heads_kernel,
        "put_heads",
        1,
        (place, *rows),
        ((TOK_DEV, TEAM * D_NOPE), (TOK_DEV, TEAM * D_ROPE)),
        [pltpu.VMEM((TEAM, TOK_DEV, D_NOPE + D_ROPE), BF16)],
    )


def side_sums(order, place, query, grad, prob, score_grad):
    part = (4, 2, PAIRS, SLICE, WIDE)
    return call(
        side_kernel,
        "key_side",
        2,
        (order, place, query, grad, prob, score_grad),
        (part, part),
        [pltpu.VMEM((2, *KEY_SHAPE), F32)],
        2**31,
        2**23,
    )


def swap(values, axes):
    return lax.all_to_all(values, axes, 0, 0, tiled=True)


def flip(values, axis):
    return lax.ppermute(values, axis, [(0, 1), (1, 0)])


def team_swap(parts):
    moved = [parts[0]]
    for ahead in range(1, TEAM):
        moved.append(lax.ppermute(parts[ahead], ("z1", "z0"), [(i, i ^ ahead) for i in range(TEAM)]))
    return moved


def local(latent, q_nope, q_rope, grad_out, w_uk, w_uv, stretch_order):
    head = lax.axis_index(PLANE + ("c",))
    places = (Z_AXES, "c", "yh", "dp")
    place = jnp.stack([lax.axis_index(axis) for axis in places]).astype(jnp.int32)

    mine = lax.dynamic_slice_in_dim(latent[0], head * SLICE, SLICE, 0)
    column = swap(jnp.broadcast_to(mine, (N_CTX, SLICE, KEY_WIDTH)), Z_AXES)
    wide = (PAIRS, SLICE, WIDE)
    first, second = column.reshape(PAIRS, 2, SLICE, KEY_WIDTH).transpose(1, 0, 2, 3)
    column = jnp.concatenate(
        [first[..., :D_LAT], second[..., :D_LAT], first[..., D_LAT:], second[..., D_LAT:]], axis=-1
    )
    own = swap(jnp.broadcast_to(column, (8, *wide)), PLANE)
    rows = team_swap(split(place, q_nope[0], q_rope[0], grad_out[0]))
    own, *rows = lax.optimization_barrier((own, *rows))
    query, grad, qn, go = prepare(stretch_order, place, rows, w_uk, w_uv)
    own = own.reshape(2, 4, *wide)
    other = flip(own, "c")

    own_keys, *own = own_scores(stretch_order, place, own, query, grad)
    keys, prob, score_grad = scores(stretch_order, place, other, query, grad, own)
    g_own, g_other = side_sums(stretch_order, place, query, grad, prob, score_grad)
    came = flip(g_other, "c")
    prob, g_own = lax.optimization_barrier((prob, g_own))
    keep, give, *rows = query_side(stretch_order, place, own_keys, keys, prob, score_grad, qn, go, w_uk)

    (pair,) = call(pair_kernel, "pair_sum", 0, (g_own, came), (g_own.shape,))
    give, pair = lax.optimization_barrier((give, pair))
    lines = swap(pair, "x")
    (weights,) = call(weight_kernel, "weight_sum", 0, (keep, flip(give, "dp")), ((N_CTX, 32, D_NOPE),))
    rows = team_swap(rows)
    lines, weights, rows = lax.optimization_barrier((lines, weights, rows))
    keep, give = call(line_kernel, "line_sum", 0, (lines,), (pair.shape[2:],) * 2)
    give, weights = lax.optimization_barrier((give, weights))
    columns = swap(weights, Z_AXES)
    came = flip(give, "yh")
    (packed,) = call(pack_kernel, "pack", 0, (columns, keep, came), ((N_CTX, SLICE, 1024 + KEY_WIDTH),))
    packed = swap(packed, Z_AXES)
    nope_grad, rope_grad = put_heads(place, rows)
    d_latent = jnp.sum(packed[:, :, 1024:].astype(F32), axis=0)
    whole = swap(jnp.broadcast_to(packed[:, :, :1024], (4, N_CTX, SLICE, 1024)), ("dp", "z0"))
    wide = (D_LAT, HEADS_DEV * D_NOPE)
    key_weight, value_weight = call(spread_kernel, "spread", 0, (whole,), (wide, wide), dtype=F32)
    return (d_latent[None], nope_grad[None], rope_grad[None], key_weight, value_weight)


def solution(mesh):
    fine = Mesh(mesh.devices.reshape(2, 4, 2, 2, 2, 4, 2), ("dp", *Z_AXES, "yh", "x", "c"))
    heads = ("yh", "x", "c")
    placed = (
        P("dp", Z_AXES, None),
        P("dp", Z_AXES, heads),
        P("dp", Z_AXES, heads),
        P("dp", Z_AXES, heads),
        P(None, heads),
        P(None, heads),
        P(),
    )
    return jax.shard_map(
        local,
        mesh=fine,
        in_specs=placed,
        out_specs=(
            P("dp", Z_AXES + heads, None),
            P("dp", Z_AXES, heads),
            P("dp", Z_AXES, heads),
            P(None, heads),
            P(None, heads),
        ),
        check_vma=False,
    )
```

```python
import math

import jax
import jax.numpy as jnp
from jax import lax
from jax.experimental import pallas as pl
from jax.experimental.pallas import tpu as pltpu
from jax.sharding import Mesh
from jax.sharding import PartitionSpec as P

D_LAT = 512
D_ROPE = 64
D_NOPE = 128
D_V = 128
KEY_WIDTH = D_LAT + D_ROPE
HEADS_DEV = 4
TOK_DEV = 128
STRETCH = 64
N_SLOT = 32
N_CTX = 16
TEAM = 4
ROWS = TEAM * STRETCH
CHUNK = 256
HALF = STRETCH // 2
PER_CHUNK = CHUNK // HALF
CHUNKS = N_SLOT // PER_CHUNK
LOW_CHUNKS = CHUNKS // 2
STEPS = CHUNKS + LOW_CHUNKS
PAIRS = N_CTX // 2
WIDE = 2 * KEY_WIDTH
QUART = TOK_DEV // 4
SLICE = 8
NEG = -1e30
SCALE = 1.0 / math.sqrt(D_NOPE + D_ROPE)
LOG2E = 1.0 / math.log(2.0)
F32 = jnp.float32
BF16 = jnp.bfloat16
Z_AXES = ("zq", "z1", "z0")
PLANE = ("yh", "x")


def dot_nt(a, b):
    return lax.dot_general(a, b, (((1,), (1,)), ((), ())), preferred_element_type=F32)


def dot_tn(a, b):
    return lax.dot_general(a, b, (((0,), (0,)), ((), ())), preferred_element_type=F32)


def dot_nn(a, b):
    return lax.dot_general(a, b, (((1,), (0,)), ((), ())), preferred_element_type=F32)


def scaled(index, unit):
    return pl.ds(pl.multiple_of(index * unit, unit), unit)


def member(place_ref, ahead):
    return (place_ref[0] % TEAM) ^ ahead


def low_half(order_ref, place_ref, ahead):
    block = place_ref[0] ^ ahead
    return jnp.where(order_ref[2 * block] > order_ref[2 * block + 1], 1, 0)


def lat_lanes(parity):
    return slice(parity * D_LAT, (parity + 1) * D_LAT)


def rope_lanes(parity):
    return slice(2 * D_LAT + parity * D_ROPE, 2 * D_LAT + (parity + 1) * D_ROPE)


def split_kernel(place_ref, qn_ref, qr_ref, go_ref, *out_refs):
    for ahead, out_ref in enumerate(out_refs):
        head = member(place_ref, ahead)
        out_ref[:TOK_DEV, :D_NOPE] = qn_ref[:, scaled(head, D_NOPE)]
        out_ref[:TOK_DEV, D_NOPE:] = go_ref[:, scaled(head, D_V)]
        two = qr_ref[:, scaled(head // 2, 2 * D_ROPE)]
        one = jnp.where(head % 2 == 1, two[:, D_ROPE:].astype(F32), two[:, :D_ROPE].astype(F32))
        out_ref[TOK_DEV:, :] = jnp.concatenate(
            [one[part * QUART : (part + 1) * QUART] for part in range(4)], axis=1
        ).astype(BF16)


def prepare_kernel(order_ref, place_ref, *refs):
    rows_refs, (wk_ref, wv_ref, query, grad, qn, go) = refs[:TEAM], refs[TEAM:]
    head = scaled(member(place_ref, 0), D_NOPE)
    wk, wv = wk_ref[:, head], wv_ref[:, head]
    nope_rows = jnp.concatenate([rows_ref[:TOK_DEV, :D_NOPE] for rows_ref in rows_refs], axis=0)
    out_rows = jnp.concatenate([rows_ref[:TOK_DEV, D_NOPE:] for rows_ref in rows_refs], axis=0)
    q_lat = dot_nt(nope_rows, wk).astype(BF16)
    g_lat = dot_nt(out_rows, wv).astype(BF16)
    for ahead, rows_ref in enumerate(rows_refs):
        late = low_half(order_ref, place_ref, ahead)
        into = slice(ahead * STRETCH, (ahead + 1) * STRETCH)
        for half in range(2):
            toks = slice(ahead * TOK_DEV + half * STRETCH, ahead * TOK_DEV + (half + 1) * STRETCH)
            rope = jnp.concatenate(
                [
                    rows_ref[TOK_DEV:, part * D_ROPE : (part + 1) * D_ROPE]
                    for part in (2 * half, 2 * half + 1)
                ],
                axis=0,
            )
            group = half ^ late
            query[group, into, :D_LAT] = q_lat[toks]
            query[group, into, D_LAT:] = rope
            grad[group, into, :] = g_lat[toks]
            qn[group, into, :] = nope_rows[toks]
            go[group, into, :] = out_rows[toks]


def step_lanes(group, chunk):
    step = chunk if group == 0 else LOW_CHUNKS + chunk
    return slice(step * CHUNK, (step + 1) * CHUNK)


def group_chunks(group):
    return LOW_CHUNKS if group == 0 else CHUNKS


def by_lane(join, values):
    return join(values[:, :128], values[:, 128:])


def half_scores(order_ref, place_ref, half, rows_ref, query, grad, keys, score, prob_grad):
    @pl.loop(0, PAIRS, unroll=4)
    def _(pair):
        for upper in range(2):
            rows = rows_ref[upper, :, pair].astype(F32).reshape(HALF, WIDE).astype(BF16)
            for parity in range(2):
                place = order_ref[4 * pair + 2 * parity + upper]
                keys[place, :, :D_LAT] = rows[:, lat_lanes(parity)]
                keys[place, :, D_LAT:] = rows[:, rope_lanes(parity)]

    col = lax.broadcasted_iota(jnp.int32, (1, CHUNK), 1)
    within = col % HALF
    core = (place_ref[1] + half) % 2
    key_pos = (col // HALF) * STRETCH + (within // SLICE) * 16 + core * SLICE + within % SLICE

    row = lax.broadcasted_iota(jnp.int32, (ROWS, 1), 0)
    row_pos = [row % STRETCH, row % STRETCH]
    for ahead in range(TEAM):
        block = place_ref[0] ^ ahead
        first, second = order_ref[2 * block], order_ref[2 * block + 1]
        mine = row // STRETCH == ahead
        row_pos[0] += jnp.where(mine, jnp.minimum(first, second) * STRETCH, 0)
        row_pos[1] += jnp.where(mine, jnp.maximum(first, second) * STRETCH, 0)

    tops = []
    for group in range(2):
        top = jnp.full((ROWS, 128), NEG, F32)
        for chunk in range(group_chunks(group)):
            lanes = step_lanes(group, chunk)
            key_rows = keys[chunk * PER_CHUNK : (chunk + 1) * PER_CHUNK].reshape(CHUNK, KEY_WIDTH)
            raw = dot_nt(query[group], key_rows) * (SCALE * LOG2E)
            if group == 0 or chunk >= LOW_CHUNKS:
                raw = jnp.where(key_pos + chunk * PER_CHUNK * STRETCH <= row_pos[group], raw, NEG)
            score[:, lanes] = raw
            prob_grad[:, lanes] = dot_nt(grad[group], key_rows[:, :D_LAT])
            top = jnp.maximum(top, by_lane(jnp.maximum, raw))
        tops.append(top)
    return tops


def own_kernel(order_ref, place_ref, own_ref, query, grad, keys, score, prob_grad, top_ref):
    tops = half_scores(order_ref, place_ref, 0, own_ref, query, grad, keys, score, prob_grad)
    for group in range(2):
        top_ref[group] = tops[group]


def score_kernel(
    order_ref,
    place_ref,
    other_ref,
    query,
    grad,
    own_score,
    own_prob_grad,
    top_ref,
    keys,
    prob_ref,
    score_grad_ref,
    score,
    prob_grad,
    expo_ref,
):
    tops = half_scores(order_ref, place_ref, 1, other_ref, query, grad, keys, score, prob_grad)
    halves = ((own_score, own_prob_grad), (score, prob_grad))
    for group in range(2):
        top = jnp.max(jnp.maximum(tops[group], top_ref[group]), axis=1, keepdims=True)
        total = jnp.zeros((ROWS, 128), F32)
        weight = jnp.zeros((ROWS, 128), F32)
        for half, (raw_ref, grad_ref) in enumerate(halves):
            for chunk in range(group_chunks(group)):
                lanes = step_lanes(group, chunk)
                expo = jnp.exp2(raw_ref[:, lanes] - top)
                expo_ref[half, :, lanes] = expo
                total += by_lane(jnp.add, expo)
                weight += by_lane(jnp.add, expo * grad_ref[:, lanes])
        inverse = 1.0 / jnp.sum(total, axis=1, keepdims=True)
        delta = jnp.sum(weight, axis=1, keepdims=True) * inverse
        for half, (raw_ref, grad_ref) in enumerate(halves):
            for chunk in range(group_chunks(group)):
                lanes = step_lanes(group, chunk)
                probability = expo_ref[half, :, lanes] * inverse
                prob_ref[half, :, lanes] = probability.astype(BF16)
                drift = grad_ref[:, lanes] - delta
                score_grad_ref[half, :, lanes] = (SCALE * probability * drift).astype(BF16)


def query_kernel(
    order_ref,
    place_ref,
    own_keys,
    other_keys,
    prob_ref,
    score_grad_ref,
    qn_ref,
    go_ref,
    wk_ref,
    keep_ref,
    give_ref,
    *refs,
):
    rows_refs, (query_low, out_low, nope) = refs[:TEAM], refs[TEAM:]
    for group in range(2):
        lanes = slice(0, LOW_CHUNKS * CHUNK) if group == 0 else slice(LOW_CHUNKS * CHUNK, STEPS * CHUNK)
        count = group_chunks(group) * PER_CHUNK
        out, query_grad = [], []
        for half, keys in enumerate((own_keys, other_keys)):
            key_rows = keys[:count].reshape(count * HALF, KEY_WIDTH)
            out.append(dot_nn(prob_ref[half, :, lanes], key_rows[:, :D_LAT]))
            query_grad.append(dot_nn(score_grad_ref[half, :, lanes], key_rows))
        out_low[group] = (out[0] + out[1]).astype(BF16)
        query_low[group] = (query_grad[0] + query_grad[1]).astype(BF16)

    wk = wk_ref[:, scaled(member(place_ref, 0), D_NOPE)]
    lat_low = query_low[:, :, :D_LAT].reshape(2 * ROWS, D_LAT)
    key_weight = dot_tn(lat_low, qn_ref[...].reshape(2 * ROWS, D_NOPE))
    value_weight = dot_tn(out_low[...].reshape(2 * ROWS, D_LAT), go_ref[...].reshape(2 * ROWS, D_V))
    even = place_ref[3] == 0
    keep_ref[...] = jnp.where(even, key_weight, value_weight).astype(BF16)
    give_ref[...] = jnp.where(even, value_weight, key_weight).astype(BF16)
    nope[...] = dot_nn(lat_low, wk).astype(BF16).reshape(2, ROWS, D_NOPE)
    for ahead, rows_ref in enumerate(rows_refs):
        late = low_half(order_ref, place_ref, ahead)
        rows = slice(ahead * STRETCH, (ahead + 1) * STRETCH)
        for half in range(2):
            group = half ^ late
            rows_ref[:STRETCH, half * D_NOPE : (half + 1) * D_NOPE] = nope[group, rows]
            rope = query_low[group, rows, D_LAT:]
            rows_ref[STRETCH:, half * 2 * D_ROPE : (half + 1) * 2 * D_ROPE] = jnp.concatenate(
                [rope[:QUART], rope[QUART:]], axis=1
            )


def heads_kernel(place_ref, *refs):
    rows_refs, (nope_ref, rope_ref, store) = refs[:TEAM], refs[TEAM:]
    for ahead, rows_ref in enumerate(rows_refs):
        store[member(place_ref, ahead)] = rows_ref[...]
    for head in range(TEAM):
        for half in range(2):
            toks = slice(half * STRETCH, (half + 1) * STRETCH)
            nope = store[head, :STRETCH, half * D_NOPE : (half + 1) * D_NOPE]
            nope_ref[toks, head * D_NOPE : (head + 1) * D_NOPE] = nope
        rope = [store[head, STRETCH:, part * D_ROPE : (part + 1) * D_ROPE] for part in range(4)]
        rope_ref[:, head * D_ROPE : (head + 1) * D_ROPE] = jnp.concatenate(rope, axis=0)


def side_kernel(
    order_ref, place_ref, query, grad, prob_ref, score_grad_ref, g_own_ref, g_other_ref, rope, slot_of
):
    for slot in range(N_SLOT):
        slot_of[order_ref[slot]] = slot
    both_query = query[...].reshape(2 * ROWS, KEY_WIDTH)
    both_grad = grad[...].reshape(2 * ROWS, D_LAT)
    for half, out_ref in enumerate((g_own_ref, g_other_ref)):
        for chunk in range(CHUNKS):
            late = step_lanes(1, chunk)
            if chunk < LOW_CHUNKS:
                early = step_lanes(0, chunk)
                score_grad, prob = [
                    jnp.concatenate([ref[half, :, early], ref[half, :, late]], axis=0)
                    for ref in (score_grad_ref, prob_ref)
                ]
                key_side, value_side = dot_tn(score_grad, both_query), dot_tn(prob, both_grad)
            else:
                key_side = dot_tn(score_grad_ref[half, :, late], query[1])
                value_side = dot_tn(prob_ref[half, :, late], grad[1])
            lat = key_side[:, :D_LAT] + value_side
            for part in range(PER_CHUNK):
                rows = slice(part * HALF, (part + 1) * HALF)
                place = chunk * PER_CHUNK + part
                slot = slot_of[place]
                apart = (slot + place_ref[2]) % 2
                lanes = scaled((slot // 2) % 2, D_LAT)
                out_ref[:, apart, slot // 4, :, lanes] = lat[rows].reshape(4, SLICE, D_LAT).astype(BF16)
                rope[half, place] = key_side[rows, D_LAT:]

    @pl.loop(0, PAIRS, unroll=4)
    def _(pair):
        for upper in range(2):
            apart = (upper + place_ref[2]) % 2
            for half, out_ref in enumerate((g_own_ref, g_other_ref)):
                both = [rope[half, order_ref[4 * pair + 2 * parity + upper]] for parity in range(2)]
                rows = jnp.concatenate(both, axis=1).reshape(4, SLICE, 2 * D_ROPE)
                out_ref[:, apart, pair, :, 2 * D_LAT :] = rows.astype(BF16)


def pair_kernel(own_ref, came_ref, out_ref):
    total = own_ref[...].astype(F32) + came_ref[...].astype(F32)
    out_ref[...] = total.astype(BF16)


def line_kernel(lines_ref, keep_ref, give_ref):
    for apart, out_ref in enumerate((keep_ref, give_ref)):
        total = lines_ref[0, apart].astype(F32)
        for source in range(1, 4):
            total += lines_ref[source, apart].astype(F32)
        out_ref[...] = total.astype(BF16)


def weight_kernel(keep_ref, came_ref, out_ref):
    total = keep_ref[...].astype(F32) + came_ref[...].astype(F32)
    out_ref[...] = total.astype(BF16).reshape(out_ref.shape)


def pack_kernel(columns_ref, keep_ref, came_ref, out_ref):
    pieces = []
    for head in range(TEAM):
        total = columns_ref[head].astype(F32)
        for source in range(head + TEAM, N_CTX, TEAM):
            total += columns_ref[source].astype(F32)
        pieces.append(total)
    for target in range(N_CTX):
        for pick in range(2):
            piece = pieces[2 * pick + target % 2]
            for octet in range(4):
                lanes = slice((4 * pick + octet) * 128, (4 * pick + octet + 1) * 128)
                out_ref[target, :, lanes] = piece[octet * SLICE : (octet + 1) * SLICE].astype(BF16)
    side = (keep_ref[...].astype(F32) + came_ref[...].astype(F32)).astype(BF16)
    for pair in range(PAIRS):
        for parity in range(2):
            out_ref[2 * pair + parity, :, 1024 : 1024 + D_LAT] = side[pair, :, lat_lanes(parity)]
            out_ref[2 * pair + parity, :, 1024 + D_LAT :] = side[pair, :, rope_lanes(parity)]


def spread_kernel(whole_ref, key_ref, value_ref):
    for corner in range(4):
        out_ref, parity = (key_ref, value_ref)[corner // 2], corner % 2
        for source in range(N_CTX):
            for pick in range(2):
                head = 2 * pick + parity
                for octet in range(4):
                    lanes = slice((4 * pick + octet) * 128, (4 * pick + octet + 1) * 128)
                    rows = slice(source * 32 + octet * SLICE, source * 32 + (octet + 1) * SLICE)
                    out_ref[rows, head * 128 : (head + 1) * 128] = whole_ref[corner, source, :, lanes].astype(F32)


VMEM = pl.BlockSpec(memory_space=pltpu.VMEM)
SMEM = pl.BlockSpec(memory_space=pltpu.SMEM)


def call(kernel, name, n_smem, args, outs, scratch=(), flops=2**20, moved=2**20, dtype=BF16):
    types = dtype if isinstance(dtype, tuple) else (dtype,) * len(outs)
    shapes = tuple(jax.ShapeDtypeStruct(shape, kind) for shape, kind in zip(outs, types))
    return pl.pallas_call(
        kernel,
        out_shape=shapes,
        in_specs=[SMEM] * n_smem + [VMEM] * (len(args) - n_smem),
        out_specs=(VMEM,) * len(outs),
        scratch_shapes=list(scratch),
        compiler_params=pltpu.CompilerParams(vmem_limit_bytes=24 * 1024 * 1024),
        cost_estimate=pl.CostEstimate(flops=flops, bytes_accessed=moved, transcendentals=0),
        name=name,
    )(*args)


QUERY_SHAPE = (2, ROWS, KEY_WIDTH)
GRAD_SHAPE = (2, ROWS, D_LAT)
HEAD_SHAPE = (2, ROWS, D_NOPE)
STEP_SHAPE = (ROWS, STEPS * CHUNK)
KEY_SHAPE = (N_SLOT, HALF, KEY_WIDTH)


def split(place, qn, qr, go):
    return call(split_kernel, "split_heads", 1, (place, qn, qr, go), ((TOK_DEV + QUART, D_NOPE + D_V),) * TEAM)


def prepare(order, place, rows, wk, wv):
    outs = (QUERY_SHAPE, GRAD_SHAPE, HEAD_SHAPE, HEAD_SHAPE)
    return call(prepare_kernel, "query_latents", 2, (order, place, *rows, wk, wv), outs, (), 2**28, 2**21)


def own_scores(order, place, own, query, grad):
    args = (order, place, own, query, grad)
    outs = (KEY_SHAPE, STEP_SHAPE, STEP_SHAPE, (2, ROWS, 128))
    return call(own_kernel, "own_scores", 2, args, outs, (), 2**30, 2**22, (BF16, F32, F32, F32))


def scores(order, place, other, query, grad, own):
    args = (order, place, other, query, grad, *own)
    outs = (KEY_SHAPE, (2, *STEP_SHAPE), (2, *STEP_SHAPE))
    scratch = [pltpu.VMEM(STEP_SHAPE, F32), pltpu.VMEM(STEP_SHAPE, F32), pltpu.VMEM((2, *STEP_SHAPE), F32)]
    return call(score_kernel, "scores", 2, args, outs, scratch, 2**31, 2**23)


def query_side(order, place, own_keys, keys, prob, score_grad, qn, go, wk):
    rows = (STRETCH + QUART, 2 * D_NOPE)
    return call(
        query_kernel,
        "query_side",
        2,
        (order, place, own_keys, keys, prob, score_grad, qn, go, wk),
        ((D_LAT, D_NOPE), (D_LAT, D_NOPE)) + (rows,) * TEAM,
        [pltpu.VMEM(QUERY_SHAPE, BF16), pltpu.VMEM(GRAD_SHAPE, BF16), pltpu.VMEM(HEAD_SHAPE, BF16)],
        2**31,
        2**23,
    )


def put_heads(place, rows):
    return call(
        heads_kernel,
        "put_heads",
        1,
        (place, *rows),
        ((TOK_DEV, TEAM * D_NOPE), (TOK_DEV, TEAM * D_ROPE)),
        [pltpu.VMEM((TEAM, STRETCH + QUART, 2 * D_NOPE), BF16)],
    )


def side_sums(order, place, query, grad, prob, score_grad):
    part = (4, 2, PAIRS, SLICE, WIDE)
    return call(
        side_kernel,
        "key_side",
        2,
        (order, place, query, grad, prob, score_grad),
        (part, part),
        [pltpu.VMEM((2, N_SLOT, HALF, D_ROPE), F32), pltpu.SMEM((N_SLOT,), jnp.int32)],
        2**31,
        2**23,
    )


def swap(values, axes):
    return lax.all_to_all(values, axes, 0, 0, tiled=True)


def flip(values, axis):
    return lax.ppermute(values, axis, [(0, 1), (1, 0)])


def team_swap(parts, mates=(2, 3, 1)):
    moved = list(parts)
    for ahead in mates:
        moved[ahead] = lax.ppermute(parts[ahead], ("z1", "z0"), [(i, i ^ ahead) for i in range(TEAM)])
    return moved


def local(latent, q_nope, q_rope, grad_out, w_uk, w_uv, stretch_order):
    head = lax.axis_index(PLANE + ("c",))
    places = (Z_AXES, "c", "yh", "dp")
    place = jnp.stack([lax.axis_index(axis) for axis in places]).astype(jnp.int32)

    mine = lax.dynamic_slice_in_dim(latent[0], head * SLICE, SLICE, 0)
    column = swap(jnp.broadcast_to(mine, (N_CTX, SLICE, KEY_WIDTH)), Z_AXES)
    wide = (PAIRS, SLICE, WIDE)
    first, second = column.reshape(PAIRS, 2, SLICE, KEY_WIDTH).transpose(1, 0, 2, 3)
    column = jnp.concatenate(
        [first[..., :D_LAT], second[..., :D_LAT], first[..., D_LAT:], second[..., D_LAT:]], axis=-1
    )
    own = swap(jnp.broadcast_to(column, (8, *wide)), PLANE)
    rows = team_swap(split(place, q_nope[0], q_rope[0], grad_out[0]))
    own, *rows = lax.optimization_barrier((own, *rows))
    query, grad, qn, go = prepare(stretch_order, place, rows, w_uk, w_uv)
    own = own.reshape(2, 4, *wide)
    other = flip(own, "c")

    own_keys, *own = own_scores(stretch_order, place, own, query, grad)
    keys, prob, score_grad = scores(stretch_order, place, other, query, grad, own)
    g_own, g_other = side_sums(stretch_order, place, query, grad, prob, score_grad)
    came = flip(g_other, "c")
    prob, g_own = lax.optimization_barrier((prob, g_own))
    keep, give, *rows = query_side(stretch_order, place, own_keys, keys, prob, score_grad, qn, go, w_uk)

    (pair,) = call(pair_kernel, "pair_sum", 0, (g_own, came), (g_own.shape,))
    give, pair = lax.optimization_barrier((give, pair))
    lines = swap(pair, "x")
    (weights,) = call(weight_kernel, "weight_sum", 0, (keep, flip(give, "dp")), ((N_CTX, 32, D_NOPE),))
    rows = team_swap(rows, (2, 3))
    lines, weights, rows = lax.optimization_barrier((lines, weights, rows))
    keep, give = call(line_kernel, "line_sum", 0, (lines,), (pair.shape[2:],) * 2)
    give, weights = lax.optimization_barrier((give, weights))
    columns = swap(weights, Z_AXES)
    came = flip(give, "yh")
    rows = team_swap(rows, (1,))
    columns, came, rows = lax.optimization_barrier((columns, came, rows))
    (packed,) = call(pack_kernel, "pack", 0, (columns, keep, came), ((N_CTX, SLICE, 1024 + KEY_WIDTH),))
    packed = swap(packed, Z_AXES)
    nope_grad, rope_grad = put_heads(place, rows)
    d_latent = jnp.sum(packed[:, :, 1024:].astype(F32), axis=0)
    whole = swap(jnp.broadcast_to(packed[:, :, :1024], (4, N_CTX, SLICE, 1024)), ("dp", "z0"))
    wide = (D_LAT, HEADS_DEV * D_NOPE)
    key_weight, value_weight = call(spread_kernel, "spread", 0, (whole,), (wide, wide), dtype=F32)
    return (d_latent[None], nope_grad[None], rope_grad[None], key_weight, value_weight)


def solution(mesh):
    fine = Mesh(mesh.devices.reshape(2, 4, 2, 2, 2, 4, 2), ("dp", *Z_AXES, "yh", "x", "c"))
    heads = ("yh", "x", "c")
    placed = (
        P("dp", Z_AXES, None),
        P("dp", Z_AXES, heads),
        P("dp", Z_AXES, heads),
        P("dp", Z_AXES, heads),
        P(None, heads),
        P(None, heads),
        P(),
    )
    return jax.shard_map(
        local,
        mesh=fine,
        in_specs=placed,
        out_specs=(
            P("dp", Z_AXES + heads, None),
            P("dp", Z_AXES, heads),
            P("dp", Z_AXES, heads),
            P(None, heads),
            P(None, heads),
        ),
        check_vma=False,
    )
```

```python
import math

import jax
import jax.numpy as jnp
from jax import lax
from jax.experimental import pallas as pl
from jax.experimental.pallas import tpu as pltpu
from jax.sharding import Mesh
from jax.sharding import PartitionSpec as P

D_LAT = 512
D_ROPE = 64
D_NOPE = 128
D_V = 128
KEY_WIDTH = D_LAT + D_ROPE
HEADS_DEV = 4
TOK_DEV = 128
STRETCH = 64
N_SLOT = 32
N_CTX = 16
TEAM = 4
ROWS = TEAM * STRETCH
CHUNK = 256
HALF = STRETCH // 2
PER_CHUNK = CHUNK // HALF
CHUNKS = N_SLOT // PER_CHUNK
LOW_CHUNKS = CHUNKS // 2
STEPS = CHUNKS + LOW_CHUNKS
PAIRS = N_CTX // 2
WIDE = 2 * KEY_WIDTH
QUART = TOK_DEV // 4
SLICE = 8
NEG = -1e30
SCALE = 1.0 / math.sqrt(D_NOPE + D_ROPE)
LOG2E = 1.0 / math.log(2.0)
F32 = jnp.float32
BF16 = jnp.bfloat16
Z_AXES = ("zq", "z1", "z0")
PLANE = ("yh", "x")


def dot_nt(a, b):
    return lax.dot_general(a, b, (((1,), (1,)), ((), ())), preferred_element_type=F32)


def dot_tn(a, b):
    return lax.dot_general(a, b, (((0,), (0,)), ((), ())), preferred_element_type=F32)


def dot_nn(a, b):
    return lax.dot_general(a, b, (((1,), (0,)), ((), ())), preferred_element_type=F32)


def scaled(index, unit):
    return pl.ds(pl.multiple_of(index * unit, unit), unit)


def member(place_ref, ahead):
    return (place_ref[0] % TEAM) ^ ahead


def low_half(order_ref, place_ref, ahead):
    block = place_ref[0] ^ ahead
    return jnp.where(order_ref[2 * block] > order_ref[2 * block + 1], 1, 0)


def lat_lanes(parity):
    return slice(parity * D_LAT, (parity + 1) * D_LAT)


def rope_lanes(parity):
    return slice(2 * D_LAT + parity * D_ROPE, 2 * D_LAT + (parity + 1) * D_ROPE)


def split_kernel(place_ref, qn_ref, qr_ref, go_ref, *out_refs):
    for ahead, out_ref in enumerate(out_refs):
        head = member(place_ref, ahead)
        out_ref[:TOK_DEV, :D_NOPE] = qn_ref[:, scaled(head, D_NOPE)]
        out_ref[:TOK_DEV, D_NOPE:] = go_ref[:, scaled(head, D_V)]
        two = qr_ref[:, scaled(head // 2, 2 * D_ROPE)]
        one = jnp.where(head % 2 == 1, two[:, D_ROPE:].astype(F32), two[:, :D_ROPE].astype(F32))
        out_ref[TOK_DEV:, :] = jnp.concatenate(
            [one[part * QUART : (part + 1) * QUART] for part in range(4)], axis=1
        ).astype(BF16)


def prepare_kernel(order_ref, place_ref, *refs):
    rows_refs, (wk_ref, wv_ref, query, grad, qn, go) = refs[:TEAM], refs[TEAM:]
    head = scaled(member(place_ref, 0), D_NOPE)
    wk, wv = wk_ref[:, head], wv_ref[:, head]
    nope_rows = jnp.concatenate([rows_ref[:TOK_DEV, :D_NOPE] for rows_ref in rows_refs], axis=0)
    out_rows = jnp.concatenate([rows_ref[:TOK_DEV, D_NOPE:] for rows_ref in rows_refs], axis=0)
    q_lat = dot_nt(nope_rows, wk).astype(BF16)
    g_lat = dot_nt(out_rows, wv).astype(BF16)
    for ahead, rows_ref in enumerate(rows_refs):
        late = low_half(order_ref, place_ref, ahead)
        into = slice(ahead * STRETCH, (ahead + 1) * STRETCH)
        for half in range(2):
            toks = slice(ahead * TOK_DEV + half * STRETCH, ahead * TOK_DEV + (half + 1) * STRETCH)
            rope = jnp.concatenate(
                [
                    rows_ref[TOK_DEV:, part * D_ROPE : (part + 1) * D_ROPE]
                    for part in (2 * half, 2 * half + 1)
                ],
                axis=0,
            )
            group = half ^ late
            query[group, into, :D_LAT] = q_lat[toks]
            query[group, into, D_LAT:] = rope
            grad[group, into, :] = g_lat[toks]
            qn[group, into, :] = nope_rows[toks]
            go[group, into, :] = out_rows[toks]


def step_lanes(group, chunk):
    step = chunk if group == 0 else LOW_CHUNKS + chunk
    return slice(step * CHUNK, (step + 1) * CHUNK)


def group_chunks(group):
    return LOW_CHUNKS if group == 0 else CHUNKS


def by_lane(join, values):
    return join(values[:, :128], values[:, 128:])


def half_scores(order_ref, place_ref, half, rows_ref, query, grad, keys, score, prob_grad):
    @pl.loop(0, PAIRS, unroll=4)
    def _(pair):
        for upper in range(2):
            rows = rows_ref[upper, :, pair].astype(F32).reshape(HALF, WIDE).astype(BF16)
            for parity in range(2):
                place = order_ref[4 * pair + 2 * parity + upper]
                keys[place, :, :D_LAT] = rows[:, lat_lanes(parity)]
                keys[place, :, D_LAT:] = rows[:, rope_lanes(parity)]

    col = lax.broadcasted_iota(jnp.int32, (1, CHUNK), 1)
    within = col % HALF
    core = (place_ref[1] + half) % 2
    key_pos = (col // HALF) * STRETCH + (within // SLICE) * 16 + core * SLICE + within % SLICE

    row = lax.broadcasted_iota(jnp.int32, (ROWS, 1), 0)
    row_pos = [row % STRETCH, row % STRETCH]
    for ahead in range(TEAM):
        block = place_ref[0] ^ ahead
        first, second = order_ref[2 * block], order_ref[2 * block + 1]
        mine = row // STRETCH == ahead
        row_pos[0] += jnp.where(mine, jnp.minimum(first, second) * STRETCH, 0)
        row_pos[1] += jnp.where(mine, jnp.maximum(first, second) * STRETCH, 0)

    tops = []
    for group in range(2):
        top = jnp.full((ROWS, 128), NEG, F32)
        for chunk in range(group_chunks(group)):
            lanes = step_lanes(group, chunk)
            key_rows = keys[chunk * PER_CHUNK : (chunk + 1) * PER_CHUNK].reshape(CHUNK, KEY_WIDTH)
            raw = dot_nt(query[group], key_rows) * (SCALE * LOG2E)
            if group == 0 or chunk >= LOW_CHUNKS:
                raw = jnp.where(key_pos + chunk * PER_CHUNK * STRETCH <= row_pos[group], raw, NEG)
            score[:, lanes] = raw
            prob_grad[:, lanes] = dot_nt(grad[group], key_rows[:, :D_LAT])
            top = jnp.maximum(top, by_lane(jnp.maximum, raw))
        tops.append(top)
    return tops


def own_kernel(order_ref, place_ref, own_ref, query, grad, keys, score, prob_grad, top_ref):
    tops = half_scores(order_ref, place_ref, 0, own_ref, query, grad, keys, score, prob_grad)
    for group in range(2):
        top_ref[group] = tops[group]


def score_kernel(
    order_ref,
    place_ref,
    other_ref,
    query,
    grad,
    own_score,
    own_prob_grad,
    top_ref,
    keys,
    prob_ref,
    score_grad_ref,
    score,
    prob_grad,
    expo_ref,
):
    tops = half_scores(order_ref, place_ref, 1, other_ref, query, grad, keys, score, prob_grad)
    halves = ((own_score, own_prob_grad), (score, prob_grad))
    for group in range(2):
        top = jnp.max(jnp.maximum(tops[group], top_ref[group]), axis=1, keepdims=True)
        total = jnp.zeros((ROWS, 128), F32)
        weight = jnp.zeros((ROWS, 128), F32)
        for half, (raw_ref, grad_ref) in enumerate(halves):
            for chunk in range(group_chunks(group)):
                lanes = step_lanes(group, chunk)
                expo = jnp.exp2(raw_ref[:, lanes] - top)
                expo_ref[half, :, lanes] = expo
                total += by_lane(jnp.add, expo)
                weight += by_lane(jnp.add, expo * grad_ref[:, lanes])
        inverse = 1.0 / jnp.sum(total, axis=1, keepdims=True)
        delta = jnp.sum(weight, axis=1, keepdims=True) * inverse
        for half, (raw_ref, grad_ref) in enumerate(halves):
            for chunk in range(group_chunks(group)):
                lanes = step_lanes(group, chunk)
                probability = expo_ref[half, :, lanes] * inverse
                prob_ref[half, :, lanes] = probability.astype(BF16)
                drift = grad_ref[:, lanes] - delta
                score_grad_ref[half, :, lanes] = (SCALE * probability * drift).astype(BF16)


def query_kernel(
    order_ref,
    place_ref,
    own_keys,
    other_keys,
    prob_ref,
    score_grad_ref,
    qn_ref,
    go_ref,
    wk_ref,
    keep_ref,
    give_ref,
    kept_ref,
    far_ref,
    near_ref,
    query_low,
    out_low,
    nope,
):
    rows_refs = (kept_ref, near_ref.at[0], far_ref, near_ref.at[1])
    for group in range(2):
        lanes = slice(0, LOW_CHUNKS * CHUNK) if group == 0 else slice(LOW_CHUNKS * CHUNK, STEPS * CHUNK)
        count = group_chunks(group) * PER_CHUNK
        out, query_grad = [], []
        for half, keys in enumerate((own_keys, other_keys)):
            key_rows = keys[:count].reshape(count * HALF, KEY_WIDTH)
            out.append(dot_nn(prob_ref[half, :, lanes], key_rows[:, :D_LAT]))
            query_grad.append(dot_nn(score_grad_ref[half, :, lanes], key_rows))
        out_low[group] = (out[0] + out[1]).astype(BF16)
        query_low[group] = (query_grad[0] + query_grad[1]).astype(BF16)

    wk = wk_ref[:, scaled(member(place_ref, 0), D_NOPE)]
    lat_low = query_low[:, :, :D_LAT].reshape(2 * ROWS, D_LAT)
    key_weight = dot_tn(lat_low, qn_ref[...].reshape(2 * ROWS, D_NOPE))
    value_weight = dot_tn(out_low[...].reshape(2 * ROWS, D_LAT), go_ref[...].reshape(2 * ROWS, D_V))
    even = place_ref[3] == 0
    keep_ref[...] = jnp.where(even, key_weight, value_weight).astype(BF16)
    give_ref[...] = jnp.where(even, value_weight, key_weight).astype(BF16)
    nope[...] = dot_nn(lat_low, wk).astype(BF16).reshape(2, ROWS, D_NOPE)
    for ahead, rows_ref in enumerate(rows_refs):
        late = low_half(order_ref, place_ref, ahead)
        rows = slice(ahead * STRETCH, (ahead + 1) * STRETCH)
        for half in range(2):
            group = half ^ late
            rows_ref[:STRETCH, half * D_NOPE : (half + 1) * D_NOPE] = nope[group, rows]
            rope = query_low[group, rows, D_LAT:]
            rows_ref[STRETCH:, half * 2 * D_ROPE : (half + 1) * 2 * D_ROPE] = jnp.concatenate(
                [rope[:QUART], rope[QUART:]], axis=1
            )


def relay_kernel(far_ref, near_ref, out_ref):
    out_ref[0] = far_ref[...]
    out_ref[1] = near_ref[1]


def heads_kernel(place_ref, kept_ref, near_ref, far_ref, nope_ref, rope_ref, store):
    for ahead, rows in enumerate((kept_ref[...], near_ref[0], far_ref[0], far_ref[1])):
        store[member(place_ref, ahead)] = rows
    for head in range(TEAM):
        for half in range(2):
            toks = slice(half * STRETCH, (half + 1) * STRETCH)
            nope = store[head, :STRETCH, half * D_NOPE : (half + 1) * D_NOPE]
            nope_ref[toks, head * D_NOPE : (head + 1) * D_NOPE] = nope
        rope = [store[head, STRETCH:, part * D_ROPE : (part + 1) * D_ROPE] for part in range(4)]
        rope_ref[:, head * D_ROPE : (head + 1) * D_ROPE] = jnp.concatenate(rope, axis=0)


def side_kernel(
    order_ref, place_ref, query, grad, prob_ref, score_grad_ref, g_own_ref, g_other_ref, rope, slot_of
):
    for slot in range(N_SLOT):
        slot_of[order_ref[slot]] = slot
    both_query = query[...].reshape(2 * ROWS, KEY_WIDTH)
    both_grad = grad[...].reshape(2 * ROWS, D_LAT)
    for half, out_ref in enumerate((g_own_ref, g_other_ref)):
        for chunk in range(CHUNKS):
            late = step_lanes(1, chunk)
            if chunk < LOW_CHUNKS:
                early = step_lanes(0, chunk)
                score_grad, prob = [
                    jnp.concatenate([ref[half, :, early], ref[half, :, late]], axis=0)
                    for ref in (score_grad_ref, prob_ref)
                ]
                key_side, value_side = dot_tn(score_grad, both_query), dot_tn(prob, both_grad)
            else:
                key_side = dot_tn(score_grad_ref[half, :, late], query[1])
                value_side = dot_tn(prob_ref[half, :, late], grad[1])
            lat = key_side[:, :D_LAT] + value_side
            for part in range(PER_CHUNK):
                rows = slice(part * HALF, (part + 1) * HALF)
                place = chunk * PER_CHUNK + part
                slot = slot_of[place]
                apart = (slot + place_ref[2]) % 2
                lanes = scaled((slot // 2) % 2, D_LAT)
                parts = lat[rows].reshape(4, SLICE, D_LAT).astype(BF16)
                for line in range(4):
                    ahead = (line + 4 - place_ref[4]) % 4
                    out_ref[ahead, apart, slot // 4, :, lanes] = parts[line]
                rope[half, place] = key_side[rows, D_LAT:]

    @pl.loop(0, PAIRS, unroll=4)
    def _(pair):
        for upper in range(2):
            apart = (upper + place_ref[2]) % 2
            for half, out_ref in enumerate((g_own_ref, g_other_ref)):
                both = [rope[half, order_ref[4 * pair + 2 * parity + upper]] for parity in range(2)]
                rows = jnp.concatenate(both, axis=1).reshape(4, SLICE, 2 * D_ROPE)
                for line in range(4):
                    ahead = (line + 4 - place_ref[4]) % 4
                    out_ref[ahead, apart, pair, :, 2 * D_LAT :] = rows[line].astype(BF16)


def pair_kernel(own_ref, came_ref, *out_refs):
    for ahead, out_ref in enumerate(out_refs):
        out_ref[...] = (own_ref[ahead].astype(F32) + came_ref[ahead].astype(F32)).astype(BF16)


def line_kernel(a_ref, b_ref, c_ref, d_ref, keep_ref, give_ref):
    for apart, out_ref in enumerate((keep_ref, give_ref)):
        total = a_ref[apart].astype(F32) + b_ref[apart].astype(F32)
        total += c_ref[apart].astype(F32) + d_ref[apart].astype(F32)
        out_ref[...] = total.astype(BF16)


def weight_kernel(keep_ref, came_ref, out_ref):
    total = keep_ref[...].astype(F32) + came_ref[...].astype(F32)
    out_ref[...] = total.astype(BF16).reshape(out_ref.shape)


def pack_kernel(columns_ref, keep_ref, came_ref, out_ref):
    pieces = []
    for head in range(TEAM):
        total = columns_ref[head].astype(F32)
        for source in range(head + TEAM, N_CTX, TEAM):
            total += columns_ref[source].astype(F32)
        pieces.append(total)
    for target in range(N_CTX):
        for pick in range(2):
            piece = pieces[2 * pick + target % 2]
            for octet in range(4):
                lanes = slice((4 * pick + octet) * 128, (4 * pick + octet + 1) * 128)
                out_ref[target, :, lanes] = piece[octet * SLICE : (octet + 1) * SLICE].astype(BF16)
    side = (keep_ref[...].astype(F32) + came_ref[...].astype(F32)).astype(BF16)
    for pair in range(PAIRS):
        for parity in range(2):
            out_ref[2 * pair + parity, :, 1024 : 1024 + D_LAT] = side[pair, :, lat_lanes(parity)]
            out_ref[2 * pair + parity, :, 1024 + D_LAT :] = side[pair, :, rope_lanes(parity)]


def spread_kernel(whole_ref, key_ref, value_ref):
    for corner in range(4):
        out_ref, parity = (key_ref, value_ref)[corner // 2], corner % 2
        for source in range(N_CTX):
            for pick in range(2):
                head = 2 * pick + parity
                for octet in range(4):
                    lanes = slice((4 * pick + octet) * 128, (4 * pick + octet + 1) * 128)
                    rows = slice(source * 32 + octet * SLICE, source * 32 + (octet + 1) * SLICE)
                    out_ref[rows, head * 128 : (head + 1) * 128] = whole_ref[corner, source, :, lanes].astype(F32)


VMEM = pl.BlockSpec(memory_space=pltpu.VMEM)
SMEM = pl.BlockSpec(memory_space=pltpu.SMEM)


def call(kernel, name, n_smem, args, outs, scratch=(), flops=2**20, moved=2**20, dtype=BF16):
    types = dtype if isinstance(dtype, tuple) else (dtype,) * len(outs)
    shapes = tuple(jax.ShapeDtypeStruct(shape, kind) for shape, kind in zip(outs, types))
    return pl.pallas_call(
        kernel,
        out_shape=shapes,
        in_specs=[SMEM] * n_smem + [VMEM] * (len(args) - n_smem),
        out_specs=(VMEM,) * len(outs),
        scratch_shapes=list(scratch),
        compiler_params=pltpu.CompilerParams(vmem_limit_bytes=24 * 1024 * 1024),
        cost_estimate=pl.CostEstimate(flops=flops, bytes_accessed=moved, transcendentals=0),
        name=name,
    )(*args)


LATE = 2**35
QUERY_SHAPE = (2, ROWS, KEY_WIDTH)
GRAD_SHAPE = (2, ROWS, D_LAT)
HEAD_SHAPE = (2, ROWS, D_NOPE)
STEP_SHAPE = (ROWS, STEPS * CHUNK)
KEY_SHAPE = (N_SLOT, HALF, KEY_WIDTH)


def split(place, qn, qr, go):
    return call(split_kernel, "split_heads", 1, (place, qn, qr, go), ((TOK_DEV + QUART, D_NOPE + D_V),) * TEAM)


def prepare(order, place, rows, wk, wv):
    outs = (QUERY_SHAPE, GRAD_SHAPE, HEAD_SHAPE, HEAD_SHAPE)
    return call(prepare_kernel, "query_latents", 2, (order, place, *rows, wk, wv), outs, (), 2**28, 2**21)


def own_scores(order, place, own, query, grad):
    args = (order, place, own, query, grad)
    outs = (KEY_SHAPE, STEP_SHAPE, STEP_SHAPE, (2, ROWS, 128))
    return call(own_kernel, "own_scores", 2, args, outs, (), 2**30, 2**22, (BF16, F32, F32, F32))


def scores(order, place, other, query, grad, own):
    args = (order, place, other, query, grad, *own)
    outs = (KEY_SHAPE, (2, *STEP_SHAPE), (2, *STEP_SHAPE))
    scratch = [pltpu.VMEM(STEP_SHAPE, F32), pltpu.VMEM(STEP_SHAPE, F32), pltpu.VMEM((2, *STEP_SHAPE), F32)]
    return call(score_kernel, "scores", 2, args, outs, scratch, 2**31, 2**23)


def query_side(order, place, own_keys, keys, prob, score_grad, qn, go, wk):
    rows = (STRETCH + QUART, 2 * D_NOPE)
    return call(
        query_kernel,
        "query_side",
        2,
        (order, place, own_keys, keys, prob, score_grad, qn, go, wk),
        ((D_LAT, D_NOPE), (D_LAT, D_NOPE), rows, rows, (2, *rows)),
        [pltpu.VMEM(QUERY_SHAPE, BF16), pltpu.VMEM(GRAD_SHAPE, BF16), pltpu.VMEM(HEAD_SHAPE, BF16)],
        2**31,
        2**23,
    )


def put_heads(place, rows):
    return call(
        heads_kernel,
        "put_heads",
        1,
        (place, *rows),
        ((TOK_DEV, TEAM * D_NOPE), (TOK_DEV, TEAM * D_ROPE)),
        [pltpu.VMEM((TEAM, STRETCH + QUART, 2 * D_NOPE), BF16)],
    )


def side_sums(order, place, query, grad, prob, score_grad):
    part = (4, 2, PAIRS, SLICE, WIDE)
    return call(
        side_kernel,
        "key_side",
        2,
        (order, place, query, grad, prob, score_grad),
        (part, part),
        [pltpu.VMEM((2, N_SLOT, HALF, D_ROPE), F32), pltpu.SMEM((N_SLOT,), jnp.int32)],
        2**31,
        2**23,
    )


def swap(values, axes):
    return lax.all_to_all(values, axes, 0, 0, tiled=True)


def flip(values, axis):
    return lax.ppermute(values, axis, [(0, 1), (1, 0)])


def team_swap(parts, mates=(2, 3, 1)):
    moved = list(parts)
    for ahead in mates:
        moved[ahead] = lax.ppermute(parts[ahead], ("z1", "z0"), [(i, i ^ ahead) for i in range(TEAM)])
    return moved


def local(latent, q_nope, q_rope, grad_out, w_uk, w_uv, stretch_order):
    head = lax.axis_index(PLANE + ("c",))
    places = (Z_AXES, "c", "yh", "dp", "x")
    place = jnp.stack([lax.axis_index(axis) for axis in places]).astype(jnp.int32)

    mine = lax.dynamic_slice_in_dim(latent[0], head * SLICE, SLICE, 0)
    column = swap(jnp.broadcast_to(mine, (N_CTX, SLICE, KEY_WIDTH)), Z_AXES)
    wide = (PAIRS, SLICE, WIDE)
    first, second = column.reshape(PAIRS, 2, SLICE, KEY_WIDTH).transpose(1, 0, 2, 3)
    column = jnp.concatenate(
        [first[..., :D_LAT], second[..., :D_LAT], first[..., D_LAT:], second[..., D_LAT:]], axis=-1
    )
    own = swap(jnp.broadcast_to(column, (8, *wide)), PLANE)
    rows = team_swap(split(place, q_nope[0], q_rope[0], grad_out[0]))
    own, *rows = lax.optimization_barrier((own, *rows))
    query, grad, qn, go = prepare(stretch_order, place, rows, w_uk, w_uv)
    own = own.reshape(2, 4, *wide)
    other = flip(own, "c")

    own_keys, *own = own_scores(stretch_order, place, own, query, grad)
    keys, prob, score_grad = scores(stretch_order, place, other, query, grad, own)
    g_own, g_other = side_sums(stretch_order, place, query, grad, prob, score_grad)
    came = flip(g_other, "c")
    prob, g_own = lax.optimization_barrier((prob, g_own))
    keep, give, kept, far, near = query_side(stretch_order, place, own_keys, keys, prob, score_grad, qn, go, w_uk)

    part = g_own.shape[1:]
    parts = call(pair_kernel, "pair_sum", 0, (g_own, came), (part,) * 4)
    give, near, *parts = lax.optimization_barrier((give, near, *parts))
    near = flip(near, "z0")
    lines = [parts[0]]
    for ahead in (2, 1, 3):
        lines.append(lax.ppermute(parts[ahead], "x", [(i, (i + ahead) % 4) for i in range(4)]))
    sums = (keep, flip(give, "dp"))
    (weights,) = call(weight_kernel, "weight_sum", 0, sums, ((N_CTX, 32, D_NOPE),), flops=LATE)
    columns = swap(weights, Z_AXES)
    keep, give = call(line_kernel, "line_sum", 0, lines, (part[1:],) * 2, flops=LATE)
    (relay,) = call(relay_kernel, "relay", 0, (far, near), (near.shape,))
    came = flip(give, "yh")
    columns, came, *rows = lax.optimization_barrier((columns, came, kept, near, flip(relay, "z1")))
    (packed,) = call(pack_kernel, "pack", 0, (columns, keep, came), ((N_CTX, SLICE, 1024 + KEY_WIDTH),))
    packed = swap(packed, Z_AXES)
    nope_grad, rope_grad = put_heads(place, rows)
    d_latent = jnp.sum(packed[:, :, 1024:].astype(F32), axis=0)
    whole = swap(jnp.broadcast_to(packed[:, :, :1024], (4, N_CTX, SLICE, 1024)), ("dp", "z0"))
    wide = (D_LAT, HEADS_DEV * D_NOPE)
    key_weight, value_weight = call(spread_kernel, "spread", 0, (whole,), (wide, wide), dtype=F32)
    return (d_latent[None], nope_grad[None], rope_grad[None], key_weight, value_weight)


def solution(mesh):
    fine = Mesh(mesh.devices.reshape(2, 4, 2, 2, 2, 4, 2), ("dp", *Z_AXES, "yh", "x", "c"))
    heads = ("yh", "x", "c")
    placed = (
        P("dp", Z_AXES, None),
        P("dp", Z_AXES, heads),
        P("dp", Z_AXES, heads),
        P("dp", Z_AXES, heads),
        P(None, heads),
        P(None, heads),
        P(),
    )
    return jax.shard_map(
        local,
        mesh=fine,
        in_specs=placed,
        out_specs=(
            P("dp", Z_AXES + heads, None),
            P("dp", Z_AXES, heads),
            P("dp", Z_AXES, heads),
            P(None, heads),
            P(None, heads),
        ),
        check_vma=False,
    )
```

```python
import math

import jax
import jax.numpy as jnp
from jax import lax
from jax.experimental import pallas as pl
from jax.experimental.pallas import tpu as pltpu
from jax.sharding import Mesh
from jax.sharding import PartitionSpec as P

D_LAT = 512
D_ROPE = 64
D_NOPE = 128
D_V = 128
KEY_WIDTH = D_LAT + D_ROPE
HEADS_DEV = 4
TOK_DEV = 128
STRETCH = 64
N_SLOT = 32
N_CTX = 16
TEAM = 4
ROWS = TEAM * STRETCH
CHUNK = 256
HALF = STRETCH // 2
PER_CHUNK = CHUNK // HALF
CHUNKS = N_SLOT // PER_CHUNK
LOW_CHUNKS = CHUNKS // 2
STEPS = CHUNKS + LOW_CHUNKS
PAIRS = N_CTX // 2
WIDE = 2 * KEY_WIDTH
QUART = TOK_DEV // 4
SLICE = 8
NEG = -1e30
SCALE = 1.0 / math.sqrt(D_NOPE + D_ROPE)
LOG2E = 1.0 / math.log(2.0)
F32 = jnp.float32
BF16 = jnp.bfloat16
Z_AXES = ("zq", "z1", "z0")
PLANE = ("yh", "x")


def dot_nt(a, b):
    return lax.dot_general(a, b, (((1,), (1,)), ((), ())), preferred_element_type=F32)


def dot_tn(a, b):
    return lax.dot_general(a, b, (((0,), (0,)), ((), ())), preferred_element_type=F32)


def dot_nn(a, b):
    return lax.dot_general(a, b, (((1,), (0,)), ((), ())), preferred_element_type=F32)


def scaled(index, unit):
    return pl.ds(pl.multiple_of(index * unit, unit), unit)


def member(place_ref, ahead):
    return (place_ref[0] % TEAM) ^ ahead


def low_half(order_ref, place_ref, ahead):
    block = place_ref[0] ^ ahead
    return jnp.where(order_ref[2 * block] > order_ref[2 * block + 1], 1, 0)


def lat_lanes(parity):
    return slice(parity * D_LAT, (parity + 1) * D_LAT)


def rope_lanes(parity):
    return slice(2 * D_LAT + parity * D_ROPE, 2 * D_LAT + (parity + 1) * D_ROPE)


def split_kernel(place_ref, qn_ref, qr_ref, go_ref, *out_refs):
    for ahead, out_ref in enumerate(out_refs):
        head = member(place_ref, ahead)
        out_ref[:TOK_DEV, :D_NOPE] = qn_ref[:, scaled(head, D_NOPE)]
        out_ref[:TOK_DEV, D_NOPE:] = go_ref[:, scaled(head, D_V)]
        two = qr_ref[:, scaled(head // 2, 2 * D_ROPE)]
        one = jnp.where(head % 2 == 1, two[:, D_ROPE:].astype(F32), two[:, :D_ROPE].astype(F32))
        out_ref[TOK_DEV:, :] = jnp.concatenate(
            [one[part * QUART : (part + 1) * QUART] for part in range(4)], axis=1
        ).astype(BF16)


def prepare_kernel(order_ref, place_ref, *refs):
    rows_refs, (wk_ref, wv_ref, query, grad, qn, go) = refs[:TEAM], refs[TEAM:]
    head = scaled(member(place_ref, 0), D_NOPE)
    wk, wv = wk_ref[:, head], wv_ref[:, head]
    nope_rows = jnp.concatenate([rows_ref[:TOK_DEV, :D_NOPE] for rows_ref in rows_refs], axis=0)
    out_rows = jnp.concatenate([rows_ref[:TOK_DEV, D_NOPE:] for rows_ref in rows_refs], axis=0)
    q_lat = dot_nt(nope_rows, wk).astype(BF16)
    g_lat = dot_nt(out_rows, wv).astype(BF16)
    for ahead, rows_ref in enumerate(rows_refs):
        late = low_half(order_ref, place_ref, ahead)
        into = slice(ahead * STRETCH, (ahead + 1) * STRETCH)
        for half in range(2):
            toks = slice(ahead * TOK_DEV + half * STRETCH, ahead * TOK_DEV + (half + 1) * STRETCH)
            rope = jnp.concatenate(
                [
                    rows_ref[TOK_DEV:, part * D_ROPE : (part + 1) * D_ROPE]
                    for part in (2 * half, 2 * half + 1)
                ],
                axis=0,
            )
            group = half ^ late
            query[group, into, :D_LAT] = q_lat[toks]
            query[group, into, D_LAT:] = rope
            grad[group, into, :] = g_lat[toks]
            qn[group, into, :] = nope_rows[toks]
            go[group, into, :] = out_rows[toks]


def step_lanes(group, chunk):
    step = chunk if group == 0 else LOW_CHUNKS + chunk
    return slice(step * CHUNK, (step + 1) * CHUNK)


def group_chunks(group):
    return LOW_CHUNKS if group == 0 else CHUNKS


def by_lane(join, values):
    return join(values[:, :128], values[:, 128:])


def half_scores(order_ref, place_ref, half, rows_ref, query, grad, keys, score, prob_grad):
    @pl.loop(0, PAIRS, unroll=4)
    def _(pair):
        for upper in range(2):
            rows = rows_ref[upper, :, pair].astype(F32).reshape(HALF, WIDE).astype(BF16)
            for parity in range(2):
                place = order_ref[4 * pair + 2 * parity + upper]
                keys[place, :, :D_LAT] = rows[:, lat_lanes(parity)]
                keys[place, :, D_LAT:] = rows[:, rope_lanes(parity)]

    col = lax.broadcasted_iota(jnp.int32, (1, CHUNK), 1)
    within = col % HALF
    core = (place_ref[1] + half) % 2
    key_pos = (col // HALF) * STRETCH + (within // SLICE) * 16 + core * SLICE + within % SLICE

    row = lax.broadcasted_iota(jnp.int32, (ROWS, 1), 0)
    row_pos = [row % STRETCH, row % STRETCH]
    for ahead in range(TEAM):
        block = place_ref[0] ^ ahead
        first, second = order_ref[2 * block], order_ref[2 * block + 1]
        mine = row // STRETCH == ahead
        row_pos[0] += jnp.where(mine, jnp.minimum(first, second) * STRETCH, 0)
        row_pos[1] += jnp.where(mine, jnp.maximum(first, second) * STRETCH, 0)

    tops = []
    for group in range(2):
        top = jnp.full((ROWS, 128), NEG, F32)
        for chunk in range(group_chunks(group)):
            lanes = step_lanes(group, chunk)
            key_rows = keys[chunk * PER_CHUNK : (chunk + 1) * PER_CHUNK].reshape(CHUNK, KEY_WIDTH)
            raw = dot_nt(query[group], key_rows) * (SCALE * LOG2E)
            if group == 0 or chunk >= LOW_CHUNKS:
                raw = jnp.where(key_pos + chunk * PER_CHUNK * STRETCH <= row_pos[group], raw, NEG)
            score[:, lanes] = raw
            prob_grad[:, lanes] = dot_nt(grad[group], key_rows[:, :D_LAT])
            top = jnp.maximum(top, by_lane(jnp.maximum, raw))
        tops.append(top)
    return tops


def own_kernel(order_ref, place_ref, own_ref, query, grad, keys, score, prob_grad, top_ref):
    tops = half_scores(order_ref, place_ref, 0, own_ref, query, grad, keys, score, prob_grad)
    for group in range(2):
        top_ref[group] = tops[group]


def score_kernel(
    order_ref,
    place_ref,
    other_ref,
    query,
    grad,
    own_score,
    own_prob_grad,
    top_ref,
    keys,
    prob_ref,
    score_grad_ref,
    score,
    prob_grad,
    expo_ref,
):
    tops = half_scores(order_ref, place_ref, 1, other_ref, query, grad, keys, score, prob_grad)
    halves = ((own_score, own_prob_grad), (score, prob_grad))
    for group in range(2):
        top = jnp.max(jnp.maximum(tops[group], top_ref[group]), axis=1, keepdims=True)
        total = jnp.zeros((ROWS, 128), F32)
        weight = jnp.zeros((ROWS, 128), F32)
        for half, (raw_ref, grad_ref) in enumerate(halves):
            for chunk in range(group_chunks(group)):
                lanes = step_lanes(group, chunk)
                expo = jnp.exp2(raw_ref[:, lanes] - top)
                expo_ref[half, :, lanes] = expo
                total += by_lane(jnp.add, expo)
                weight += by_lane(jnp.add, expo * grad_ref[:, lanes])
        inverse = 1.0 / jnp.sum(total, axis=1, keepdims=True)
        delta = jnp.sum(weight, axis=1, keepdims=True) * inverse
        for half, (raw_ref, grad_ref) in enumerate(halves):
            for chunk in range(group_chunks(group)):
                lanes = step_lanes(group, chunk)
                probability = expo_ref[half, :, lanes] * inverse
                prob_ref[half, :, lanes] = probability.astype(BF16)
                drift = grad_ref[:, lanes] - delta
                score_grad_ref[half, :, lanes] = (SCALE * probability * drift).astype(BF16)


def query_kernel(
    order_ref,
    place_ref,
    own_keys,
    other_keys,
    prob_ref,
    score_grad_ref,
    qn_ref,
    go_ref,
    wk_ref,
    keep_ref,
    give_ref,
    kept_ref,
    far_ref,
    near_ref,
    query_low,
    out_low,
    nope,
):
    rows_refs = (kept_ref, near_ref.at[0], far_ref, near_ref.at[1])
    for group in range(2):
        lanes = slice(0, LOW_CHUNKS * CHUNK) if group == 0 else slice(LOW_CHUNKS * CHUNK, STEPS * CHUNK)
        count = group_chunks(group) * PER_CHUNK
        out, query_grad = [], []
        for half, keys in enumerate((own_keys, other_keys)):
            key_rows = keys[:count].reshape(count * HALF, KEY_WIDTH)
            out.append(dot_nn(prob_ref[half, :, lanes], key_rows[:, :D_LAT]))
            query_grad.append(dot_nn(score_grad_ref[half, :, lanes], key_rows))
        out_low[group] = (out[0] + out[1]).astype(BF16)
        query_low[group] = (query_grad[0] + query_grad[1]).astype(BF16)

    wk = wk_ref[:, scaled(member(place_ref, 0), D_NOPE)]
    lat_low = query_low[:, :, :D_LAT].reshape(2 * ROWS, D_LAT)
    key_weight = dot_tn(lat_low, qn_ref[...].reshape(2 * ROWS, D_NOPE))
    value_weight = dot_tn(out_low[...].reshape(2 * ROWS, D_LAT), go_ref[...].reshape(2 * ROWS, D_V))
    even = place_ref[3] == 0
    keep_ref[...] = jnp.where(even, key_weight, value_weight).astype(BF16)
    give_ref[...] = jnp.where(even, value_weight, key_weight).astype(BF16)
    nope[...] = dot_nn(lat_low, wk).astype(BF16).reshape(2, ROWS, D_NOPE)
    for ahead, rows_ref in enumerate(rows_refs):
        late = low_half(order_ref, place_ref, ahead)
        rows = slice(ahead * STRETCH, (ahead + 1) * STRETCH)
        for half in range(2):
            group = half ^ late
            rows_ref[:STRETCH, half * D_NOPE : (half + 1) * D_NOPE] = nope[group, rows]
            rope = query_low[group, rows, D_LAT:]
            rows_ref[STRETCH:, half * 2 * D_ROPE : (half + 1) * 2 * D_ROPE] = jnp.concatenate(
                [rope[:QUART], rope[QUART:]], axis=1
            )


def relay_kernel(far_ref, near_ref, out_ref):
    out_ref[0] = far_ref[...]
    out_ref[1] = near_ref[1]


def heads_kernel(place_ref, kept_ref, near_ref, far_ref, nope_ref, rope_ref, store):
    for ahead, rows in enumerate((kept_ref[...], near_ref[0], far_ref[0], far_ref[1])):
        store[member(place_ref, ahead)] = rows
    for head in range(TEAM):
        for half in range(2):
            toks = slice(half * STRETCH, (half + 1) * STRETCH)
            nope = store[head, :STRETCH, half * D_NOPE : (half + 1) * D_NOPE]
            nope_ref[toks, head * D_NOPE : (head + 1) * D_NOPE] = nope
        rope = [store[head, STRETCH:, part * D_ROPE : (part + 1) * D_ROPE] for part in range(4)]
        rope_ref[:, head * D_ROPE : (head + 1) * D_ROPE] = jnp.concatenate(rope, axis=0)


def side_kernel(
    order_ref, place_ref, query, grad, prob_ref, score_grad_ref, g_own_ref, g_other_ref, rope, slot_of
):
    for slot in range(N_SLOT):
        slot_of[order_ref[slot]] = slot
    both_query = query[...].reshape(2 * ROWS, KEY_WIDTH)
    both_grad = grad[...].reshape(2 * ROWS, D_LAT)
    for half, out_ref in enumerate((g_own_ref, g_other_ref)):
        for chunk in range(CHUNKS):
            late = step_lanes(1, chunk)
            if chunk < LOW_CHUNKS:
                early = step_lanes(0, chunk)
                score_grad, prob = [
                    jnp.concatenate([ref[half, :, early], ref[half, :, late]], axis=0)
                    for ref in (score_grad_ref, prob_ref)
                ]
                key_side, value_side = dot_tn(score_grad, both_query), dot_tn(prob, both_grad)
            else:
                key_side = dot_tn(score_grad_ref[half, :, late], query[1])
                value_side = dot_tn(prob_ref[half, :, late], grad[1])
            lat = key_side[:, :D_LAT] + value_side
            for part in range(PER_CHUNK):
                rows = slice(part * HALF, (part + 1) * HALF)
                place = chunk * PER_CHUNK + part
                slot = slot_of[place]
                apart = (slot + place_ref[2]) % 2
                lanes = scaled((slot // 2) % 2, D_LAT)
                parts = lat[rows].reshape(4, SLICE, D_LAT).astype(BF16)
                for line in range(4):
                    ahead = line ^ place_ref[4]
                    out_ref[ahead % 2, ahead // 2, apart, slot // 4, :, lanes] = parts[line]
                rope[half, place] = key_side[rows, D_LAT:]

    @pl.loop(0, PAIRS, unroll=4)
    def _(pair):
        for upper in range(2):
            apart = (upper + place_ref[2]) % 2
            for half, out_ref in enumerate((g_own_ref, g_other_ref)):
                both = [rope[half, order_ref[4 * pair + 2 * parity + upper]] for parity in range(2)]
                rows = jnp.concatenate(both, axis=1).reshape(4, SLICE, 2 * D_ROPE)
                for line in range(4):
                    ahead = line ^ place_ref[4]
                    out_ref[ahead % 2, ahead // 2, apart, pair, :, 2 * D_LAT :] = rows[line].astype(BF16)


def pair_kernel(own_ref, came_ref, *out_refs):
    for ahead, out_ref in enumerate(out_refs):
        out_ref[...] = (own_ref[ahead].astype(F32) + came_ref[ahead].astype(F32)).astype(BF16)


def line_kernel(keep_ref, came_ref, *out_refs):
    for index, out_ref in enumerate(out_refs):
        across, apart = index // 2, index % 2
        total = keep_ref[across, apart].astype(F32) + came_ref[across, apart].astype(F32)
        out_ref[...] = total.astype(BF16)


def weight_kernel(keep_ref, came_ref, out_ref):
    total = keep_ref[...].astype(F32) + came_ref[...].astype(F32)
    out_ref[...] = total.astype(BF16).reshape(out_ref.shape)


def pack_kernel(columns_ref, a_ref, b_ref, c_ref, d_ref, out_ref):
    pieces = []
    for head in range(TEAM):
        total = columns_ref[head].astype(F32)
        for source in range(head + TEAM, N_CTX, TEAM):
            total += columns_ref[source].astype(F32)
        pieces.append(total)
    for target in range(N_CTX):
        for pick in range(2):
            piece = pieces[2 * pick + target % 2]
            for octet in range(4):
                lanes = slice((4 * pick + octet) * 128, (4 * pick + octet + 1) * 128)
                out_ref[target, :, lanes] = piece[octet * SLICE : (octet + 1) * SLICE].astype(BF16)
    side = a_ref[...].astype(F32) + b_ref[...].astype(F32)
    side = (side + c_ref[...].astype(F32) + d_ref[...].astype(F32)).astype(BF16)
    for pair in range(PAIRS):
        for parity in range(2):
            out_ref[2 * pair + parity, :, 1024 : 1024 + D_LAT] = side[pair, :, lat_lanes(parity)]
            out_ref[2 * pair + parity, :, 1024 + D_LAT :] = side[pair, :, rope_lanes(parity)]


def spread_kernel(whole_ref, key_ref, value_ref):
    for corner in range(4):
        out_ref, parity = (key_ref, value_ref)[corner // 2], corner % 2
        for source in range(N_CTX):
            for pick in range(2):
                head = 2 * pick + parity
                for octet in range(4):
                    lanes = slice((4 * pick + octet) * 128, (4 * pick + octet + 1) * 128)
                    rows = slice(source * 32 + octet * SLICE, source * 32 + (octet + 1) * SLICE)
                    out_ref[rows, head * 128 : (head + 1) * 128] = whole_ref[corner, source, :, lanes].astype(F32)


VMEM = pl.BlockSpec(memory_space=pltpu.VMEM)
SMEM = pl.BlockSpec(memory_space=pltpu.SMEM)


def call(kernel, name, n_smem, args, outs, scratch=(), flops=2**20, moved=2**20, dtype=BF16):
    types = dtype if isinstance(dtype, tuple) else (dtype,) * len(outs)
    shapes = tuple(jax.ShapeDtypeStruct(shape, kind) for shape, kind in zip(outs, types))
    return pl.pallas_call(
        kernel,
        out_shape=shapes,
        in_specs=[SMEM] * n_smem + [VMEM] * (len(args) - n_smem),
        out_specs=(VMEM,) * len(outs),
        scratch_shapes=list(scratch),
        compiler_params=pltpu.CompilerParams(vmem_limit_bytes=24 * 1024 * 1024),
        cost_estimate=pl.CostEstimate(flops=flops, bytes_accessed=moved, transcendentals=0),
        name=name,
    )(*args)


LATE = 2**35
QUERY_SHAPE = (2, ROWS, KEY_WIDTH)
GRAD_SHAPE = (2, ROWS, D_LAT)
HEAD_SHAPE = (2, ROWS, D_NOPE)
STEP_SHAPE = (ROWS, STEPS * CHUNK)
KEY_SHAPE = (N_SLOT, HALF, KEY_WIDTH)


def split(place, qn, qr, go):
    return call(split_kernel, "split_heads", 1, (place, qn, qr, go), ((TOK_DEV + QUART, D_NOPE + D_V),) * TEAM)


def prepare(order, place, rows, wk, wv):
    outs = (QUERY_SHAPE, GRAD_SHAPE, HEAD_SHAPE, HEAD_SHAPE)
    return call(prepare_kernel, "query_latents", 2, (order, place, *rows, wk, wv), outs, (), 2**28, 2**21)


def own_scores(order, place, own, query, grad):
    args = (order, place, own, query, grad)
    outs = (KEY_SHAPE, STEP_SHAPE, STEP_SHAPE, (2, ROWS, 128))
    return call(own_kernel, "own_scores", 2, args, outs, (), 2**30, 2**22, (BF16, F32, F32, F32))


def scores(order, place, other, query, grad, own):
    args = (order, place, other, query, grad, *own)
    outs = (KEY_SHAPE, (2, *STEP_SHAPE), (2, *STEP_SHAPE))
    scratch = [pltpu.VMEM(STEP_SHAPE, F32), pltpu.VMEM(STEP_SHAPE, F32), pltpu.VMEM((2, *STEP_SHAPE), F32)]
    return call(score_kernel, "scores", 2, args, outs, scratch, 2**31, 2**23)


def query_side(order, place, own_keys, keys, prob, score_grad, qn, go, wk):
    rows = (STRETCH + QUART, 2 * D_NOPE)
    return call(
        query_kernel,
        "query_side",
        2,
        (order, place, own_keys, keys, prob, score_grad, qn, go, wk),
        ((D_LAT, D_NOPE), (D_LAT, D_NOPE), rows, rows, (2, *rows)),
        [pltpu.VMEM(QUERY_SHAPE, BF16), pltpu.VMEM(GRAD_SHAPE, BF16), pltpu.VMEM(HEAD_SHAPE, BF16)],
        2**31,
        2**23,
    )


def put_heads(place, rows):
    return call(
        heads_kernel,
        "put_heads",
        1,
        (place, *rows),
        ((TOK_DEV, TEAM * D_NOPE), (TOK_DEV, TEAM * D_ROPE)),
        [pltpu.VMEM((TEAM, STRETCH + QUART, 2 * D_NOPE), BF16)],
    )


def side_sums(order, place, query, grad, prob, score_grad):
    part = (2, 2, 2, PAIRS, SLICE, WIDE)
    return call(
        side_kernel,
        "key_side",
        2,
        (order, place, query, grad, prob, score_grad),
        (part, part),
        [pltpu.VMEM((2, N_SLOT, HALF, D_ROPE), F32), pltpu.SMEM((N_SLOT,), jnp.int32)],
        2**31,
        2**23,
    )


def swap(values, axes):
    return lax.all_to_all(values, axes, 0, 0, tiled=True)


def flip(values, axis):
    return lax.ppermute(values, axis, [(0, 1), (1, 0)])


def team_swap(parts, mates=(2, 3, 1)):
    moved = list(parts)
    for ahead in mates:
        moved[ahead] = lax.ppermute(parts[ahead], ("z1", "z0"), [(i, i ^ ahead) for i in range(TEAM)])
    return moved


def local(latent, q_nope, q_rope, grad_out, w_uk, w_uv, stretch_order):
    head = lax.axis_index(PLANE + ("c",))
    places = (Z_AXES, "c", "yh", "dp", "x")
    place = jnp.stack([lax.axis_index(axis) for axis in places]).astype(jnp.int32)

    mine = lax.dynamic_slice_in_dim(latent[0], head * SLICE, SLICE, 0)
    column = swap(jnp.broadcast_to(mine, (N_CTX, SLICE, KEY_WIDTH)), Z_AXES)
    wide = (PAIRS, SLICE, WIDE)
    first, second = column.reshape(PAIRS, 2, SLICE, KEY_WIDTH).transpose(1, 0, 2, 3)
    column = jnp.concatenate(
        [first[..., :D_LAT], second[..., :D_LAT], first[..., D_LAT:], second[..., D_LAT:]], axis=-1
    )
    own = swap(jnp.broadcast_to(column, (8, *wide)), PLANE)
    rows = team_swap(split(place, q_nope[0], q_rope[0], grad_out[0]))
    own, *rows = lax.optimization_barrier((own, *rows))
    query, grad, qn, go = prepare(stretch_order, place, rows, w_uk, w_uv)
    own = own.reshape(2, 4, *wide)
    other = flip(own, "c")

    own_keys, *own = own_scores(stretch_order, place, own, query, grad)
    keys, prob, score_grad = scores(stretch_order, place, other, query, grad, own)
    g_own, g_other = side_sums(stretch_order, place, query, grad, prob, score_grad)
    came = flip(g_other, "c")
    prob, g_own = lax.optimization_barrier((prob, g_own))
    keep, give, kept, far, near = query_side(stretch_order, place, own_keys, keys, prob, score_grad, qn, go, w_uk)

    part = g_own.shape[1:]
    parts = call(pair_kernel, "pair_sum", 0, (g_own, came), (part,) * 2)
    give, near, *parts = lax.optimization_barrier((give, near, *parts))
    beside = lax.ppermute(parts[1], "x", [(i, i ^ 1) for i in range(4)])
    near = flip(near, "z0")
    sums = (keep, flip(give, "dp"))
    (weights,) = call(weight_kernel, "weight_sum", 0, sums, ((N_CTX, 32, D_NOPE),), flops=LATE)
    columns = swap(weights, Z_AXES)
    lines = call(line_kernel, "line_sum", 0, (parts[0], beside), (part[2:],) * 4, flops=LATE)
    (relay,) = call(relay_kernel, "relay", 0, (far, near), (near.shape,))
    sides = [lines[0]]
    for ahead, share in ((6, lines[3]), (2, lines[2]), (4, lines[1])):
        sides.append(lax.ppermute(share, PLANE, [(i, i ^ ahead) for i in range(8)]))
    columns, *rest = lax.optimization_barrier((columns, *sides, kept, near, flip(relay, "z1")))
    sides, rows = rest[:4], rest[4:]
    (packed,) = call(pack_kernel, "pack", 0, (columns, *sides), ((N_CTX, SLICE, 1024 + KEY_WIDTH),))
    packed = swap(packed, Z_AXES)
    nope_grad, rope_grad = put_heads(place, rows)
    d_latent = jnp.sum(packed[:, :, 1024:].astype(F32), axis=0)
    whole = swap(jnp.broadcast_to(packed[:, :, :1024], (4, N_CTX, SLICE, 1024)), ("dp", "z0"))
    wide = (D_LAT, HEADS_DEV * D_NOPE)
    key_weight, value_weight = call(spread_kernel, "spread", 0, (whole,), (wide, wide), dtype=F32)
    return (d_latent[None], nope_grad[None], rope_grad[None], key_weight, value_weight)


def solution(mesh):
    fine = Mesh(mesh.devices.reshape(2, 4, 2, 2, 2, 4, 2), ("dp", *Z_AXES, "yh", "x", "c"))
    heads = ("yh", "x", "c")
    placed = (
        P("dp", Z_AXES, None),
        P("dp", Z_AXES, heads),
        P("dp", Z_AXES, heads),
        P("dp", Z_AXES, heads),
        P(None, heads),
        P(None, heads),
        P(),
    )
    return jax.shard_map(
        local,
        mesh=fine,
        in_specs=placed,
        out_specs=(
            P("dp", Z_AXES + heads, None),
            P("dp", Z_AXES, heads),
            P("dp", Z_AXES, heads),
            P(None, heads),
            P(None, heads),
        ),
        check_vma=False,
    )
```

```python
import math

import jax
import jax.numpy as jnp
from jax import lax
from jax.experimental import pallas as pl
from jax.experimental.pallas import tpu as pltpu
from jax.sharding import Mesh
from jax.sharding import PartitionSpec as P

D_LAT = 512
D_ROPE = 64
D_NOPE = 128
D_V = 128
KEY_WIDTH = D_LAT + D_ROPE
HEADS_DEV = 4
TOK_DEV = 128
STRETCH = 64
N_SLOT = 32
N_CTX = 16
TEAM = 4
ROWS = TEAM * STRETCH
CHUNK = 256
HALF = STRETCH // 2
PER_CHUNK = CHUNK // HALF
CHUNKS = N_SLOT // PER_CHUNK
LOW_CHUNKS = CHUNKS // 2
STEPS = CHUNKS + LOW_CHUNKS
PAIRS = N_CTX // 2
WIDE = 2 * KEY_WIDTH
QUART = TOK_DEV // 4
SLICE = 8
NEG = -1e30
SCALE = 1.0 / math.sqrt(D_NOPE + D_ROPE)
LOG2E = 1.0 / math.log(2.0)
F32 = jnp.float32
BF16 = jnp.bfloat16
Z_AXES = ("zq", "z1", "z0")
PLANE = ("yh", "x")


def dot_nt(a, b):
    return lax.dot_general(a, b, (((1,), (1,)), ((), ())), preferred_element_type=F32)


def dot_tn(a, b):
    return lax.dot_general(a, b, (((0,), (0,)), ((), ())), preferred_element_type=F32)


def dot_nn(a, b):
    return lax.dot_general(a, b, (((1,), (0,)), ((), ())), preferred_element_type=F32)


def scaled(index, unit):
    return pl.ds(pl.multiple_of(index * unit, unit), unit)


def member(place_ref, ahead):
    return (place_ref[0] % TEAM) ^ ahead


def low_half(order_ref, place_ref, ahead):
    block = place_ref[0] ^ ahead
    return jnp.where(order_ref[2 * block] > order_ref[2 * block + 1], 1, 0)


def lat_lanes(parity):
    return slice(parity * D_LAT, (parity + 1) * D_LAT)


def rope_lanes(parity):
    return slice(2 * D_LAT + parity * D_ROPE, 2 * D_LAT + (parity + 1) * D_ROPE)


def split_kernel(place_ref, qn_ref, qr_ref, go_ref, *out_refs):
    for ahead, out_ref in enumerate(out_refs):
        head = member(place_ref, ahead)
        out_ref[:TOK_DEV, :D_NOPE] = qn_ref[:, scaled(head, D_NOPE)]
        out_ref[:TOK_DEV, D_NOPE:] = go_ref[:, scaled(head, D_V)]
        two = qr_ref[:, scaled(head // 2, 2 * D_ROPE)]
        one = jnp.where(head % 2 == 1, two[:, D_ROPE:].astype(F32), two[:, :D_ROPE].astype(F32))
        out_ref[TOK_DEV:, :] = jnp.concatenate(
            [one[part * QUART : (part + 1) * QUART] for part in range(4)], axis=1
        ).astype(BF16)


def prepare_kernel(order_ref, place_ref, *refs):
    rows_refs, (wk_ref, wv_ref, query, grad, qn, go) = refs[:TEAM], refs[TEAM:]
    head = scaled(member(place_ref, 0), D_NOPE)
    wk, wv = wk_ref[:, head], wv_ref[:, head]
    nope_rows = jnp.concatenate([rows_ref[:TOK_DEV, :D_NOPE] for rows_ref in rows_refs], axis=0)
    out_rows = jnp.concatenate([rows_ref[:TOK_DEV, D_NOPE:] for rows_ref in rows_refs], axis=0)
    q_lat = dot_nt(nope_rows, wk).astype(BF16)
    g_lat = dot_nt(out_rows, wv).astype(BF16)
    for ahead, rows_ref in enumerate(rows_refs):
        late = low_half(order_ref, place_ref, ahead)
        into = slice(ahead * STRETCH, (ahead + 1) * STRETCH)
        for half in range(2):
            toks = slice(ahead * TOK_DEV + half * STRETCH, ahead * TOK_DEV + (half + 1) * STRETCH)
            rope = jnp.concatenate(
                [
                    rows_ref[TOK_DEV:, part * D_ROPE : (part + 1) * D_ROPE]
                    for part in (2 * half, 2 * half + 1)
                ],
                axis=0,
            )
            group = half ^ late
            query[group, into, :D_LAT] = q_lat[toks]
            query[group, into, D_LAT:] = rope
            grad[group, into, :] = g_lat[toks]
            qn[group, into, :] = nope_rows[toks]
            go[group, into, :] = out_rows[toks]


def step_lanes(group, chunk):
    step = chunk if group == 0 else LOW_CHUNKS + chunk
    return slice(step * CHUNK, (step + 1) * CHUNK)


def group_chunks(group):
    return LOW_CHUNKS if group == 0 else CHUNKS


def by_lane(join, values):
    return join(values[:, :128], values[:, 128:])


def half_scores(order_ref, place_ref, half, rows_ref, query, grad, keys, score, prob_grad):
    @pl.loop(0, PAIRS, unroll=4)
    def _(pair):
        for upper in range(2):
            rows = rows_ref[upper, :, pair].astype(F32).reshape(HALF, WIDE).astype(BF16)
            for parity in range(2):
                place = order_ref[4 * pair + 2 * parity + upper]
                keys[place, :, :D_LAT] = rows[:, lat_lanes(parity)]
                keys[place, :, D_LAT:] = rows[:, rope_lanes(parity)]

    col = lax.broadcasted_iota(jnp.int32, (1, CHUNK), 1)
    within = col % HALF
    core = (place_ref[1] + half) % 2
    key_pos = (col // HALF) * STRETCH + (within // SLICE) * 16 + core * SLICE + within % SLICE

    row = lax.broadcasted_iota(jnp.int32, (ROWS, 1), 0)
    row_pos = [row % STRETCH, row % STRETCH]
    for ahead in range(TEAM):
        block = place_ref[0] ^ ahead
        first, second = order_ref[2 * block], order_ref[2 * block + 1]
        mine = row // STRETCH == ahead
        row_pos[0] += jnp.where(mine, jnp.minimum(first, second) * STRETCH, 0)
        row_pos[1] += jnp.where(mine, jnp.maximum(first, second) * STRETCH, 0)

    tops = []
    for group in range(2):
        top = jnp.full((ROWS, 128), NEG, F32)
        for chunk in range(group_chunks(group)):
            lanes = step_lanes(group, chunk)
            key_rows = keys[chunk * PER_CHUNK : (chunk + 1) * PER_CHUNK].reshape(CHUNK, KEY_WIDTH)
            raw = dot_nt(query[group], key_rows) * (SCALE * LOG2E)
            if group == 0 or chunk >= LOW_CHUNKS:
                raw = jnp.where(key_pos + chunk * PER_CHUNK * STRETCH <= row_pos[group], raw, NEG)
            score[:, lanes] = raw
            prob_grad[:, lanes] = dot_nt(grad[group], key_rows[:, :D_LAT])
            top = jnp.maximum(top, by_lane(jnp.maximum, raw))
        tops.append(top)
    return tops


def own_kernel(order_ref, place_ref, own_ref, query, grad, keys, score, prob_grad, top_ref):
    tops = half_scores(order_ref, place_ref, 0, own_ref, query, grad, keys, score, prob_grad)
    for group in range(2):
        top_ref[group] = tops[group]


def score_kernel(
    order_ref,
    place_ref,
    other_ref,
    query,
    grad,
    own_score,
    own_prob_grad,
    top_ref,
    keys,
    prob_ref,
    score_grad_ref,
    score,
    prob_grad,
    expo_ref,
):
    tops = half_scores(order_ref, place_ref, 1, other_ref, query, grad, keys, score, prob_grad)
    halves = ((own_score, own_prob_grad), (score, prob_grad))
    for group in range(2):
        top = jnp.max(jnp.maximum(tops[group], top_ref[group]), axis=1, keepdims=True)
        total = jnp.zeros((ROWS, 128), F32)
        weight = jnp.zeros((ROWS, 128), F32)
        for half, (raw_ref, grad_ref) in enumerate(halves):
            for chunk in range(group_chunks(group)):
                lanes = step_lanes(group, chunk)
                expo = jnp.exp2(raw_ref[:, lanes] - top)
                expo_ref[half, :, lanes] = expo
                total += by_lane(jnp.add, expo)
                weight += by_lane(jnp.add, expo * grad_ref[:, lanes])
        inverse = 1.0 / jnp.sum(total, axis=1, keepdims=True)
        delta = jnp.sum(weight, axis=1, keepdims=True) * inverse
        for half, (raw_ref, grad_ref) in enumerate(halves):
            for chunk in range(group_chunks(group)):
                lanes = step_lanes(group, chunk)
                probability = expo_ref[half, :, lanes] * inverse
                prob_ref[half, :, lanes] = probability.astype(BF16)
                drift = grad_ref[:, lanes] - delta
                score_grad_ref[half, :, lanes] = (SCALE * probability * drift).astype(BF16)


def query_kernel(
    order_ref,
    place_ref,
    own_keys,
    other_keys,
    prob_ref,
    score_grad_ref,
    qn_ref,
    go_ref,
    wk_ref,
    keep_ref,
    give_ref,
    kept_ref,
    far_ref,
    near_ref,
    query_low,
    out_low,
    nope,
):
    rows_refs = (kept_ref, near_ref.at[0], far_ref, near_ref.at[1])
    for group in range(2):
        lanes = slice(0, LOW_CHUNKS * CHUNK) if group == 0 else slice(LOW_CHUNKS * CHUNK, STEPS * CHUNK)
        count = group_chunks(group) * PER_CHUNK
        out, query_grad = [], []
        for half, keys in enumerate((own_keys, other_keys)):
            key_rows = keys[:count].reshape(count * HALF, KEY_WIDTH)
            out.append(dot_nn(prob_ref[half, :, lanes], key_rows[:, :D_LAT]))
            query_grad.append(dot_nn(score_grad_ref[half, :, lanes], key_rows))
        out_low[group] = (out[0] + out[1]).astype(BF16)
        query_low[group] = (query_grad[0] + query_grad[1]).astype(BF16)

    wk = wk_ref[:, scaled(member(place_ref, 0), D_NOPE)]
    lat_low = query_low[:, :, :D_LAT].reshape(2 * ROWS, D_LAT)
    key_weight = dot_tn(lat_low, qn_ref[...].reshape(2 * ROWS, D_NOPE))
    value_weight = dot_tn(out_low[...].reshape(2 * ROWS, D_LAT), go_ref[...].reshape(2 * ROWS, D_V))
    even = place_ref[3] == 0
    keep_ref[...] = jnp.where(even, key_weight, value_weight).astype(BF16)
    give_ref[...] = jnp.where(even, value_weight, key_weight).astype(BF16)
    nope[...] = dot_nn(lat_low, wk).astype(BF16).reshape(2, ROWS, D_NOPE)
    for ahead, rows_ref in enumerate(rows_refs):
        late = low_half(order_ref, place_ref, ahead)
        rows = slice(ahead * STRETCH, (ahead + 1) * STRETCH)
        for half in range(2):
            group = half ^ late
            rows_ref[:STRETCH, half * D_NOPE : (half + 1) * D_NOPE] = nope[group, rows]
            rope = query_low[group, rows, D_LAT:]
            rows_ref[STRETCH:, half * 2 * D_ROPE : (half + 1) * 2 * D_ROPE] = jnp.concatenate(
                [rope[:QUART], rope[QUART:]], axis=1
            )


def relay_kernel(far_ref, near_ref, out_ref):
    out_ref[0] = far_ref[...]
    out_ref[1] = near_ref[1]


def heads_kernel(place_ref, kept_ref, near_ref, far_ref, nope_ref, rope_ref, store):
    for ahead, rows in enumerate((kept_ref[...], near_ref[0], far_ref[0], far_ref[1])):
        store[member(place_ref, ahead)] = rows
    for head in range(TEAM):
        for half in range(2):
            toks = slice(half * STRETCH, (half + 1) * STRETCH)
            nope = store[head, :STRETCH, half * D_NOPE : (half + 1) * D_NOPE]
            nope_ref[toks, head * D_NOPE : (head + 1) * D_NOPE] = nope
        rope = [store[head, STRETCH:, part * D_ROPE : (part + 1) * D_ROPE] for part in range(4)]
        rope_ref[:, head * D_ROPE : (head + 1) * D_ROPE] = jnp.concatenate(rope, axis=0)


def side_kernel(
    order_ref, place_ref, query, grad, prob_ref, score_grad_ref, g_own_ref, g_other_ref, rope, slot_of
):
    for slot in range(N_SLOT):
        slot_of[order_ref[slot]] = slot
    both_query = query[...].reshape(2 * ROWS, KEY_WIDTH)
    both_grad = grad[...].reshape(2 * ROWS, D_LAT)
    for half, out_ref in enumerate((g_own_ref, g_other_ref)):
        for chunk in range(CHUNKS):
            late = step_lanes(1, chunk)
            if chunk < LOW_CHUNKS:
                early = step_lanes(0, chunk)
                score_grad, prob = [
                    jnp.concatenate([ref[half, :, early], ref[half, :, late]], axis=0)
                    for ref in (score_grad_ref, prob_ref)
                ]
                key_side, value_side = dot_tn(score_grad, both_query), dot_tn(prob, both_grad)
            else:
                key_side = dot_tn(score_grad_ref[half, :, late], query[1])
                value_side = dot_tn(prob_ref[half, :, late], grad[1])
            lat = key_side[:, :D_LAT] + value_side
            for part in range(PER_CHUNK):
                rows = slice(part * HALF, (part + 1) * HALF)
                place = chunk * PER_CHUNK + part
                slot = slot_of[place]
                apart = (slot + place_ref[2]) % 2
                lanes = scaled((slot // 2) % 2, D_LAT)
                parts = lat[rows].reshape(4, SLICE, D_LAT).astype(BF16)
                for line in range(4):
                    ahead = line ^ place_ref[4]
                    out_ref[ahead % 2, ahead // 2, apart, slot // 4, :, lanes] = parts[line]
                rope[half, place] = key_side[rows, D_LAT:]

    @pl.loop(0, PAIRS, unroll=4)
    def _(pair):
        for upper in range(2):
            apart = (upper + place_ref[2]) % 2
            for half, out_ref in enumerate((g_own_ref, g_other_ref)):
                both = [rope[half, order_ref[4 * pair + 2 * parity + upper]] for parity in range(2)]
                rows = jnp.concatenate(both, axis=1).reshape(4, SLICE, 2 * D_ROPE)
                for line in range(4):
                    ahead = line ^ place_ref[4]
                    out_ref[ahead % 2, ahead // 2, apart, pair, :, 2 * D_LAT :] = rows[line].astype(BF16)


def pair_kernel(own_ref, came_ref, *out_refs):
    for ahead, out_ref in enumerate(out_refs):
        out_ref[...] = (own_ref[ahead].astype(F32) + came_ref[ahead].astype(F32)).astype(BF16)


def line_kernel(keep_ref, came_ref, *out_refs):
    for index, out_ref in enumerate(out_refs):
        across, apart = index // 2, index % 2
        total = keep_ref[across, apart].astype(F32) + came_ref[across, apart].astype(F32)
        out_ref[...] = total.astype(BF16)


def weight_kernel(keep_ref, came_ref, out_ref):
    total = keep_ref[...].astype(F32) + came_ref[...].astype(F32)
    out_ref[...] = total.astype(BF16).reshape(out_ref.shape)


def pack_kernel(columns_ref, a_ref, b_ref, c_ref, d_ref, out_ref):
    pieces = []
    for head in range(TEAM):
        total = columns_ref[head].astype(F32)
        for source in range(head + TEAM, N_CTX, TEAM):
            total += columns_ref[source].astype(F32)
        pieces.append(total)
    for target in range(N_CTX):
        for pick in range(2):
            piece = pieces[2 * pick + target % 2]
            for octet in range(4):
                lanes = slice((4 * pick + octet) * 128, (4 * pick + octet + 1) * 128)
                out_ref[target, :, lanes] = piece[octet * SLICE : (octet + 1) * SLICE].astype(BF16)
    side = a_ref[...].astype(F32) + b_ref[...].astype(F32)
    side = (side + c_ref[...].astype(F32) + d_ref[...].astype(F32)).astype(BF16)
    for pair in range(PAIRS):
        for parity in range(2):
            out_ref[2 * pair + parity, :, 1024 : 1024 + D_LAT] = side[pair, :, lat_lanes(parity)]
            out_ref[2 * pair + parity, :, 1024 + D_LAT :] = side[pair, :, rope_lanes(parity)]


def spread_kernel(whole_ref, key_ref, value_ref):
    for corner in range(4):
        out_ref, parity = (key_ref, value_ref)[corner // 2], corner % 2
        for source in range(N_CTX):
            for pick in range(2):
                head = 2 * pick + parity
                for octet in range(4):
                    lanes = slice((4 * pick + octet) * 128, (4 * pick + octet + 1) * 128)
                    rows = slice(source * 32 + octet * SLICE, source * 32 + (octet + 1) * SLICE)
                    out_ref[rows, head * 128 : (head + 1) * 128] = whole_ref[corner, source, :, lanes].astype(F32)


VMEM = pl.BlockSpec(memory_space=pltpu.VMEM)
SMEM = pl.BlockSpec(memory_space=pltpu.SMEM)


def call(kernel, name, n_smem, args, outs, scratch=(), flops=2**20, moved=2**20, dtype=BF16):
    types = dtype if isinstance(dtype, tuple) else (dtype,) * len(outs)
    shapes = tuple(jax.ShapeDtypeStruct(shape, kind) for shape, kind in zip(outs, types))
    return pl.pallas_call(
        kernel,
        out_shape=shapes,
        in_specs=[SMEM] * n_smem + [VMEM] * (len(args) - n_smem),
        out_specs=(VMEM,) * len(outs),
        scratch_shapes=list(scratch),
        compiler_params=pltpu.CompilerParams(vmem_limit_bytes=24 * 1024 * 1024),
        cost_estimate=pl.CostEstimate(flops=flops, bytes_accessed=moved, transcendentals=0),
        name=name,
    )(*args)


LATE = 2**35
QUERY_SHAPE = (2, ROWS, KEY_WIDTH)
GRAD_SHAPE = (2, ROWS, D_LAT)
HEAD_SHAPE = (2, ROWS, D_NOPE)
STEP_SHAPE = (ROWS, STEPS * CHUNK)
KEY_SHAPE = (N_SLOT, HALF, KEY_WIDTH)


def split(place, qn, qr, go):
    return call(split_kernel, "split_heads", 1, (place, qn, qr, go), ((TOK_DEV + QUART, D_NOPE + D_V),) * TEAM)


def prepare(order, place, rows, wk, wv):
    outs = (QUERY_SHAPE, GRAD_SHAPE, HEAD_SHAPE, HEAD_SHAPE)
    return call(prepare_kernel, "query_latents", 2, (order, place, *rows, wk, wv), outs, (), 2**28, 2**21)


def own_scores(order, place, own, query, grad):
    args = (order, place, own, query, grad)
    outs = (KEY_SHAPE, STEP_SHAPE, STEP_SHAPE, (2, ROWS, 128))
    return call(own_kernel, "own_scores", 2, args, outs, (), 2**30, 2**22, (BF16, F32, F32, F32))


def scores(order, place, other, query, grad, own):
    args = (order, place, other, query, grad, *own)
    outs = (KEY_SHAPE, (2, *STEP_SHAPE), (2, *STEP_SHAPE))
    scratch = [pltpu.VMEM(STEP_SHAPE, F32), pltpu.VMEM(STEP_SHAPE, F32), pltpu.VMEM((2, *STEP_SHAPE), F32)]
    return call(score_kernel, "scores", 2, args, outs, scratch, 2**31, 2**23)


def query_side(order, place, own_keys, keys, prob, score_grad, qn, go, wk):
    rows = (STRETCH + QUART, 2 * D_NOPE)
    return call(
        query_kernel,
        "query_side",
        2,
        (order, place, own_keys, keys, prob, score_grad, qn, go, wk),
        ((D_LAT, D_NOPE), (D_LAT, D_NOPE), rows, rows, (2, *rows)),
        [pltpu.VMEM(QUERY_SHAPE, BF16), pltpu.VMEM(GRAD_SHAPE, BF16), pltpu.VMEM(HEAD_SHAPE, BF16)],
        2**31,
        2**23,
    )


def put_heads(place, rows):
    return call(
        heads_kernel,
        "put_heads",
        1,
        (place, *rows),
        ((TOK_DEV, TEAM * D_NOPE), (TOK_DEV, TEAM * D_ROPE)),
        [pltpu.VMEM((TEAM, STRETCH + QUART, 2 * D_NOPE), BF16)],
    )


def side_sums(order, place, query, grad, prob, score_grad):
    part = (2, 2, 2, PAIRS, SLICE, WIDE)
    return call(
        side_kernel,
        "key_side",
        2,
        (order, place, query, grad, prob, score_grad),
        (part, part),
        [pltpu.VMEM((2, N_SLOT, HALF, D_ROPE), F32), pltpu.SMEM((N_SLOT,), jnp.int32)],
        2**31,
        2**23,
    )


def swap(values, axes):
    return lax.all_to_all(values, axes, 0, 0, tiled=True)


def flip(values, axis):
    return lax.ppermute(values, axis, [(0, 1), (1, 0)])


def team_swap(parts, mates=(2, 3, 1)):
    moved = list(parts)
    for ahead in mates:
        moved[ahead] = lax.ppermute(parts[ahead], ("z1", "z0"), [(i, i ^ ahead) for i in range(TEAM)])
    return moved


def local(latent, q_nope, q_rope, grad_out, w_uk, w_uv, stretch_order):
    head = lax.axis_index(PLANE + ("c",))
    places = (Z_AXES, "c", "yh", "dp", "x")
    place = jnp.stack([lax.axis_index(axis) for axis in places]).astype(jnp.int32)

    mine = lax.dynamic_slice_in_dim(latent[0], head * SLICE, SLICE, 0)
    column = swap(jnp.broadcast_to(mine, (N_CTX, SLICE, KEY_WIDTH)), Z_AXES)
    wide = (PAIRS, SLICE, WIDE)
    first, second = column.reshape(PAIRS, 2, SLICE, KEY_WIDTH).transpose(1, 0, 2, 3)
    column = jnp.concatenate(
        [first[..., :D_LAT], second[..., :D_LAT], first[..., D_LAT:], second[..., D_LAT:]], axis=-1
    )
    own = swap(jnp.broadcast_to(column, (8, *wide)), PLANE)
    rows = team_swap(split(place, q_nope[0], q_rope[0], grad_out[0]))
    own, *rows = lax.optimization_barrier((own, *rows))
    query, grad, qn, go = prepare(stretch_order, place, rows, w_uk, w_uv)
    own = own.reshape(2, 4, *wide)
    other = flip(own, "c")

    own_keys, *own = own_scores(stretch_order, place, own, query, grad)
    keys, prob, score_grad = scores(stretch_order, place, other, query, grad, own)
    g_own, g_other = side_sums(stretch_order, place, query, grad, prob, score_grad)
    came = flip(g_other, "c")
    prob, g_own = lax.optimization_barrier((prob, g_own))
    keep, give, kept, far, near = query_side(stretch_order, place, own_keys, keys, prob, score_grad, qn, go, w_uk)

    part = g_own.shape[1:]
    parts = call(pair_kernel, "pair_sum", 0, (g_own, came), (part,) * 2)
    give, near, *parts = lax.optimization_barrier((give, near, *parts))
    beside = lax.ppermute(parts[1], "x", [(i, i ^ 1) for i in range(4)])
    near = flip(near, "z0")
    sums = (keep, flip(give, "dp"))
    (weights,) = call(weight_kernel, "weight_sum", 0, sums, ((N_CTX, 32, D_NOPE),))
    columns = swap(weights, Z_AXES)
    lines = call(line_kernel, "line_sum", 0, (parts[0], beside), (part[2:],) * 4, flops=LATE)
    (relay,) = call(relay_kernel, "relay", 0, (far, near), (near.shape,))
    sides = [lines[0]]
    for ahead, share in ((6, lines[3]), (2, lines[2]), (4, lines[1])):
        sides.append(lax.ppermute(share, PLANE, [(i, i ^ ahead) for i in range(8)]))
    columns, *rest = lax.optimization_barrier((columns, *sides, kept, near, flip(relay, "z1")))
    sides, rows = rest[:4], rest[4:]
    (packed,) = call(pack_kernel, "pack", 0, (columns, *sides), ((N_CTX, SLICE, 1024 + KEY_WIDTH),))
    packed = swap(packed, Z_AXES)
    nope_grad, rope_grad = put_heads(place, rows)
    d_latent = jnp.sum(packed[:, :, 1024:].astype(F32), axis=0)
    whole = swap(jnp.broadcast_to(packed[:, :, :1024], (4, N_CTX, SLICE, 1024)), ("dp", "z0"))
    wide = (D_LAT, HEADS_DEV * D_NOPE)
    key_weight, value_weight = call(spread_kernel, "spread", 0, (whole,), (wide, wide), dtype=F32)
    return (d_latent[None], nope_grad[None], rope_grad[None], key_weight, value_weight)


def solution(mesh):
    fine = Mesh(mesh.devices.reshape(2, 4, 2, 2, 2, 4, 2), ("dp", *Z_AXES, "yh", "x", "c"))
    heads = ("yh", "x", "c")
    placed = (
        P("dp", Z_AXES, None),
        P("dp", Z_AXES, heads),
        P("dp", Z_AXES, heads),
        P("dp", Z_AXES, heads),
        P(None, heads),
        P(None, heads),
        P(),
    )
    return jax.shard_map(
        local,
        mesh=fine,
        in_specs=placed,
        out_specs=(
            P("dp", Z_AXES + heads, None),
            P("dp", Z_AXES, heads),
            P("dp", Z_AXES, heads),
            P(None, heads),
            P(None, heads),
        ),
        check_vma=False,
    )
```
